512 devices in a mesh: site: 8 (over y), sector: 64 (over z, x, core).
Axes of the slice: x: 4, y: 8, z: 8, core: 2. Of those that a mesh axis runs over, the one named last changes fastest.
Arguments:
- site_blocks: bfloat16 [8, 64, 4, 256, 256], P('site', 'sector'), may hold values from -0.375 to 0.375
- operators: float32 [8, 4, 4, 4], P('site'), may hold values from -2.5 to 2.5
- op_mask: int32 [8, 4, 4, 4], P('site'), may hold values 0 or 1
- coupling: int32 [8, 64, 4], P('site', 'sector'), may hold values 0 or 1
- start_env: bfloat16 [64, 4, 256, 256], P('sector'), may hold values from -6 to 6
Outputs:
- left_envs: bfloat16 [8, 64, 4, 256, 256], P('site', 'sector')
The draws below stay inside these ranges and needn't reach their ends.
All inputs are finite; a program needn't handle non-finite values. No bound on the sum of `op_mask` or of `coupling` on one device may be relied on, other than what follows from the above.
Results may differ from the reference program's by a relative error of at most 0.034.
Values may be sent and summed in bfloat16 or wider, within the bound.
No kernel may reach another device: no remote copies, remote signals or barrier semaphores. Data moves between devices by JAX's collectives and lax.ppermute only.
A program may use at most 64 MiB of HBM per device.

```python
import jax
import jax.numpy as jnp
from jax import lax

B = 256
CH = 4
STATES = 4
SITES = 8
SECTORS = 64


def plant(values, stream_key, low, high):
    shape = values.shape
    index_at = [jax.random.randint(jax.random.fold_in(stream_key, axis), (), 0, shape[axis]) for axis in range(len(shape))]
    values = values.at[tuple(index_at)].set(low)
    longest = shape.index(max(shape))
    index_at[longest] = (index_at[longest] + 1) % shape[longest]
    return values.at[tuple(index_at)].set(high)


def level_of(own_key, dims, split, least, top_value):
    def one(axis_at, shards_of):
        steps = jax.random.uniform(jax.random.fold_in(jax.random.fold_in(own_key, 6), axis_at), (shards_of,), jnp.float32, least / len(split), top_value / len(split))
        return jnp.repeat(jnp.exp(steps), dims[axis_at] // shards_of).reshape((-1,) + (1,) * (len(dims) - axis_at - 1))

    factor_of = one(*split[0])
    for cut in split[1:]:
        factor_of = factor_of * one(*cut)
    return factor_of


def noise(stream_key, shape, deviation, reach, split=(), held_as=jnp.bfloat16):
    loudness = level_of(stream_key, shape, split, -0.22, 0.18) if split else 1.0
    entries = jax.random.normal(stream_key, shape, jnp.float32) * deviation * loudness
    return jnp.minimum(jnp.maximum(entries, -reach), reach).astype(held_as)


def setup_inputs(seed: int = 0) -> dict:
    streams_of = jax.random.split(jax.random.key(seed), 6)
    site_blocks = noise(streams_of[0], (SITES, SECTORS, STATES, B, B), B ** -0.5, 0.375, ((0, 8), (1, 64)))
    operators = noise(streams_of[1], (SITES, CH, CH, STATES), 6 ** -0.5, 2.5, ((0, 8),), jnp.float32)
    op_mask = plant((jax.random.randint(streams_of[2], (SITES, CH, CH, STATES), 0, 2) < 1).astype(jnp.int32), jax.random.fold_in(streams_of[2], 1), 0, 1)
    coupling = plant((jax.random.randint(streams_of[3], (SITES, SECTORS, STATES), 0, 4) < 3).astype(jnp.int32), jax.random.fold_in(streams_of[3], 1), 0, 1)
    start_env = noise(streams_of[4], (SECTORS, CH, B, B), 1.0, 6.0, ((0, 64),))
    return dict(site_blocks=site_blocks, operators=operators, op_mask=op_mask, coupling=coupling, start_env=start_env)


def reference(site_blocks, operators, op_mask, coupling, start_env):
    highest = lax.Precision.HIGHEST
    current = start_env.astype(jnp.float32)
    stored = [None] * SITES
    for position in range(SITES):
        weights = operators[position] * op_mask[position].astype(jnp.float32)
        coupled = coupling[position].astype(jnp.float32)
        mixed_ops = jnp.einsum("wvp,qwij,qp->qpvij", weights, current, coupled, precision=highest)
        mixed_ops = lax.optimization_barrier(mixed_ops.astype(jnp.bfloat16)).astype(jnp.float32)
        blocks = site_blocks[position].astype(jnp.float32)
        half_done = jnp.einsum("qpvij,qpjk->qpvik", mixed_ops, blocks, precision=highest)
        half_done = lax.optimization_barrier(half_done.astype(jnp.bfloat16)).astype(jnp.float32)
        keep_full = jnp.einsum("qji,qvjk->qvik", blocks[:, 0], half_done[:, 0], precision=highest)
        next_full = jnp.einsum("qpji,qpvjk->qvik", blocks[:, 1:3], half_done[:, 1:3], precision=highest)
        skip_full = jnp.einsum("qji,qvjk->qvik", blocks[:, 3], half_done[:, 3], precision=highest)
        keep_part = lax.optimization_barrier(keep_full.astype(jnp.bfloat16)).astype(jnp.float32)
        next_part = lax.optimization_barrier(next_full.astype(jnp.bfloat16)).astype(jnp.float32)
        skip_part = lax.optimization_barrier(skip_full.astype(jnp.bfloat16)).astype(jnp.float32)
        zero_one = jnp.zeros_like(next_part[:1])
        zero_two = jnp.zeros_like(skip_part[:2])
        summed = keep_part + jnp.concatenate([zero_one, next_part[:-1]], axis=0)
        summed = summed + jnp.concatenate([zero_two, skip_part[:-2]], axis=0)
        fresh = summed.astype(jnp.bfloat16)
        stored[(position + 1) % SITES] = fresh
        current = lax.optimization_barrier(fresh).astype(jnp.float32)
    return jnp.stack(stored)
```

```python
import functools

import jax
import jax.numpy as jnp
from jax import lax
from jax.experimental import pallas as pl
from jax.experimental.pallas import tpu as pltpu
from jax.sharding import PartitionSpec as P

AXES = ("site", "sector")
RING = 8
ROUND = (8, 7)


def moved(x, pairs, sectors):
    flat = [(a * sectors + b, c * sectors + d) for (a, b), (c, d) in pairs]
    return lax.ppermute(x, AXES, flat)


def mix_and_multiply(env_ref, a_ref, w_ref, p, mixed_ref, half_ref):
    size = env_ref.shape[-1]
    step = 32
    for i in range(0, size, step):
        rows = [env_ref[w, i : i + step, :].astype(jnp.float32) for w in range(4)]
        for v in range(4):
            total = rows[0] * w_ref[p * 16 + v * 4]
            for w in range(1, 4):
                total = total + rows[w] * w_ref[p * 16 + v * 4 + w]
            mixed_ref[v * size + i : v * size + i + step, :] = total.astype(jnp.bfloat16)
    block = a_ref[pl.ds(pl.multiple_of(p * size, size), size), :]
    half_ref[...] = jnp.dot(
        mixed_ref[...], block, preferred_element_type=jnp.float32
    ).astype(jnp.bfloat16)
    return block


def close(block, half):
    return lax.dot_general(
        block, half, (((0,), (0,)), ((), ())), preferred_element_type=jnp.float32
    )


def one_unit(env_ref, a_ref, w_ref, p, mixed_ref, half_ref, out_ref):
    size = env_ref.shape[-1]
    block = mix_and_multiply(env_ref, a_ref, w_ref, p, mixed_ref, half_ref)
    for v in range(4):
        half = half_ref[v * size : (v + 1) * size, :]
        out_ref[v] = close(block, half).astype(jnp.bfloat16)


def unit_kernel(p_ref, w_ref, env_ref, a_ref, out_ref, mixed_ref, half_ref):
    one_unit(env_ref, a_ref, w_ref, p_ref[0], mixed_ref, half_ref, out_ref)


def pair_kernel(w_ref, env_ref, a_ref, out_ref, mixed_ref, half_ref, mixed2_ref, half2_ref):
    size = env_ref.shape[-1]
    first = mix_and_multiply(env_ref, a_ref, w_ref, 1, mixed_ref, half_ref)
    second = mix_and_multiply(env_ref, a_ref, w_ref, 2, mixed2_ref, half2_ref)
    for v in range(4):
        at = slice(v * size, (v + 1) * size)
        total = close(first, half_ref[at, :]) + close(second, half2_ref[at, :])
        out_ref[v] = total.astype(jnp.bfloat16)


def summed(turn, own_ref, over_ref, swap_ref, edge_ref, env_ref):
    size = env_ref.shape[-1]
    step = 32

    def add(one_ref):
        for v in range(4):
            for i in range(0, size, step):
                at = (v, slice(i, i + step))
                total = (
                    swap_ref[at].astype(jnp.float32)
                    + one_ref[at].astype(jnp.float32)
                    + edge_ref[at].astype(jnp.float32)
                )
                env_ref[at] = total.astype(jnp.bfloat16)

    @pl.when(turn == 1)
    def _():
        add(over_ref)

    @pl.when(turn == 0)
    def _():
        add(own_ref)


def lead_kernel(
    p_ref, w_ref, own_ref, over_ref, swap_ref, edge_ref, a_ref, env_ref, out_ref, mixed_ref, half_ref
):
    summed(p_ref[1], own_ref, over_ref, swap_ref, edge_ref, env_ref)
    one_unit(env_ref, a_ref, w_ref, p_ref[0], mixed_ref, half_ref, out_ref)


def last_kernel(p_ref, own_ref, over_ref, swap_ref, edge_ref, near_ref, far_ref, out_ref, sem):
    @pl.when(p_ref[0] == 0)
    def _():
        summed(p_ref[1], own_ref, over_ref, swap_ref, edge_ref, out_ref)

    @pl.when(p_ref[0] == 1)
    def _():
        copy = pltpu.make_async_copy(near_ref, out_ref, sem)
        copy.start()
        copy.wait()

    @pl.when(p_ref[0] == 2)
    def _():
        copy = pltpu.make_async_copy(far_ref, out_ref, sem)
        copy.start()
        copy.wait()


def pick_kernel(count, p_ref, *refs):
    out_ref, sem = refs[count], refs[count + 1]
    for i in range(count):

        @pl.when(p_ref[0] == i)
        def _():
            copy = pltpu.make_async_copy(refs[i], out_ref, sem)
            copy.start()
            copy.wait()


VMEM = pl.BlockSpec(memory_space=pltpu.VMEM)
SMEM = pl.BlockSpec(memory_space=pltpu.SMEM)
ANY = pl.BlockSpec(memory_space=pl.ANY)
PARAMS = pltpu.CompilerParams(vmem_limit_bytes=24 * 1024 * 1024)


def scratch(count, channels, size):
    return [pltpu.VMEM((channels * size, size), jnp.bfloat16)] * count


def cost(units, arrays):
    return pl.CostEstimate(
        flops=units * 8 * 2 * 256**3, bytes_accessed=arrays * 2**19, transcendentals=0
    )


def local(site_blocks, operators, op_mask, coupling, start_env):
    sites = lax.axis_size("site")
    sectors = lax.axis_size("sector")
    lines = sectors // RING
    row = lax.axis_index("site")
    place = lax.axis_index("sector")
    slot = lax.rem(place, RING)
    odd = lax.rem(place, 2)
    states, size = site_blocks.shape[2], site_blocks.shape[3]
    block_shape = jax.ShapeDtypeStruct(start_env.shape[1:], jnp.bfloat16)
    channels = start_env.shape[1]

    def at(line, slot_at):
        return line * RING + slot_at % RING

    coupled = coupling[0, 0].astype(jnp.float32)
    weights = operators[0] * op_mask[0].astype(jnp.float32) * coupled[None, None, :]
    weights = weights.transpose(2, 1, 0).reshape(-1)
    high = lax.reduce_precision(weights, *ROUND)
    middle = lax.reduce_precision(weights - high, *ROUND)
    low = lax.reduce_precision(weights - high - middle, *ROUND)
    pieces = jnp.stack([high, middle, low]).astype(jnp.bfloat16)
    pieces = jnp.pad(pieces, ((0, 13), (0, size - pieces.shape[1])))
    blocks = site_blocks[0, 0].reshape(states * size, size)
    packed = jnp.concatenate([blocks, pieces], axis=0)

    def weights_of(parcel):
        parts = parcel[states * size : states * size + 3, : weights.shape[0]].astype(jnp.float32)
        return parts[0] + parts[1] + parts[2]

    lane = [(line, u) for line in range(lines) for u in range(RING)]
    parcels = [None] * sites
    parcels[1] = moved(
        packed, [((1, at(z, u)), (0, at(z, u - 1))) for z, u in lane], sectors
    )
    turned = moved(
        packed,
        [((s, at(z, u)), (s, at(z, u - s))) for s in range(2, sites) for z, u in lane],
        sectors,
    )

    def fetch(s, after):
        held, after = lax.optimization_barrier((turned, after))
        pairs = [((s, q), (0, q)) for q in range(sectors)]
        return moved(held, pairs, sectors), after

    def edge_pairs(s):
        pairs = []
        for z, v in lane:
            u = (v + s) % RING
            if v % 2 == 0:
                pairs.append(((0, at(z, v)), (0, at(z, v - 1))))
            elif z + (u >= 6) < lines:
                pairs.append(((0, at(z, v)), (0, at(z + (u >= 6), v + 1))))
        return pairs

    def swap_pairs(s):
        pairs = []
        for z, v in lane:
            u = (v + s) % RING
            if v % 2 == 1:
                pairs.append(((0, at(z, v)), (0, at(z, v - 1))))
            elif z + (u >= 6) < lines:
                pairs.append(((0, at(z, v)), (0, at(z + (u >= 6), v + 1))))
        return pairs

    def over_pairs(s):
        v = (RING - 1 - s) % RING
        return [((0, at(z, v)), (0, at(z + 1, v))) for z in range(lines - 1)]

    edge_state = jnp.stack([3 * odd])
    swap_state = jnp.stack([3 * (1 - odd)])
    current = start_env[0]
    kept = {}
    for s in range(sites):
        if s == 0:
            parcel, scales = blocks, weights
            edge = pl.pallas_call(
                unit_kernel,
                out_shape=block_shape,
                in_specs=[SMEM, SMEM, VMEM, VMEM],
                out_specs=VMEM,
                scratch_shapes=scratch(2, channels, size),
                compiler_params=PARAMS,
                cost_estimate=cost(1, 4),
                name="first",
            )(edge_state, scales, current, parcel)
        else:
            parcel = parcels[s]
            scales = weights_of(parcel)
            turn = (lax.rem(slot + s - 1, RING) == RING - 1).astype(jnp.int32)
            current, edge = pl.pallas_call(
                lead_kernel,
                out_shape=(block_shape, block_shape),
                in_specs=[SMEM, SMEM, VMEM, VMEM, VMEM, VMEM, VMEM],
                out_specs=(VMEM, VMEM),
                scratch_shapes=scratch(2, channels, size),
                compiler_params=PARAMS,
                cost_estimate=cost(1, 6),
                name="lead",
            )(jnp.stack([3 * odd, turn]), scales, own, over, swap, edge_in, parcel)
            kept[s] = current
        edge_in = moved(edge, edge_pairs(s), sectors)
        inner = pl.pallas_call(
            unit_kernel,
            out_shape=block_shape,
            in_specs=[SMEM, SMEM, VMEM, VMEM],
            out_specs=VMEM,
            scratch_shapes=scratch(2, channels, size),
            compiler_params=PARAMS,
            cost_estimate=cost(1, 4),
            name="inner",
        )(swap_state, scales, current, parcel)
        swap = moved(inner, swap_pairs(s), sectors)
        own = pl.pallas_call(
            pair_kernel,
            out_shape=block_shape,
            in_specs=[SMEM, VMEM, VMEM],
            out_specs=VMEM,
            scratch_shapes=scratch(4, channels, size),
            compiler_params=PARAMS,
            cost_estimate=cost(2, 4),
            name="stay",
        )(scales, current, parcel)
        over = moved(own, over_pairs(s), sectors)
        for ahead in ([2, 3] if s == 0 else [s + 3]):
            if ahead < sites:
                parcels[ahead], own = fetch(ahead, own)

    near = min(6, sites)
    raised = [
        moved(kept[r], [((0, q), (r, q)) for q in range(sectors)], sectors)
        for r in range(1, near)
    ]
    picked = pl.pallas_call(
        functools.partial(pick_kernel, len(raised)),
        out_shape=block_shape,
        in_specs=[SMEM] + [ANY] * len(raised),
        out_specs=ANY,
        scratch_shapes=[pltpu.SemaphoreType.DMA],
        name="pick",
    )(jnp.stack([row - 1]), *raised)
    homeward = moved(
        picked,
        [((r, at(z, u - r)), (r, at(z, u))) for r in range(1, near) for z, u in lane],
        sectors,
    )
    direct = [
        moved(kept[r], [((0, at(z, u - r)), (r, at(z, u))) for z, u in lane], sectors)
        for r in range(near, sites)
    ]
    straight = pl.pallas_call(
        functools.partial(pick_kernel, len(direct)),
        out_shape=block_shape,
        in_specs=[SMEM] + [ANY] * len(direct),
        out_specs=ANY,
        scratch_shapes=[pltpu.SemaphoreType.DMA],
        name="pick_late",
    )(jnp.stack([row - near]), *direct)
    turn = (lax.rem(slot + sites - 1, RING) == RING - 1).astype(jnp.int32)
    kind = jnp.where(row == 0, 0, jnp.where(row < near, 1, 2))
    out = pl.pallas_call(
        last_kernel,
        out_shape=block_shape,
        in_specs=[SMEM] + [VMEM] * 4 + [ANY] * 2,
        out_specs=VMEM,
        scratch_shapes=[pltpu.SemaphoreType.DMA],
        compiler_params=PARAMS,
        name="last",
    )(jnp.stack([kind, turn]), own, over, swap, edge_in, homeward, straight)
    return out[None, None]


def solution(mesh):
    return jax.shard_map(
        local,
        mesh=mesh,
        in_specs=(
            P("site", "sector", None, None, None),
            P("site", None, None, None),
            P("site", None, None, None),
            P("site", "sector", None),
            P("sector", None, None, None),
        ),
        out_specs=P("site", "sector", None, None, None),
        check_vma=False,
    )
```

```python
import functools

import jax
import jax.numpy as jnp
from jax import lax
from jax.experimental import pallas as pl
from jax.experimental.pallas import tpu as pltpu
from jax.sharding import PartitionSpec as P

AXES = ("site", "sector")
RING = 8
ROUND = (8, 7)


def moved(x, pairs, sectors):
    flat = [(a * sectors + b, c * sectors + d) for (a, b), (c, d) in pairs]
    return lax.ppermute(x, AXES, flat)


def mix_and_multiply(env_ref, a_ref, w_ref, p, mixed_ref, half_ref):
    size = env_ref.shape[-1]
    step = 32
    for i in range(0, size, step):
        rows = [env_ref[w, i : i + step, :].astype(jnp.float32) for w in range(4)]
        for v in range(4):
            total = rows[0] * w_ref[p * 16 + v * 4]
            for w in range(1, 4):
                total = total + rows[w] * w_ref[p * 16 + v * 4 + w]
            mixed_ref[v * size + i : v * size + i + step, :] = total.astype(jnp.bfloat16)
    block = a_ref[pl.ds(pl.multiple_of(p * size, size), size), :]
    half_ref[...] = jnp.dot(
        mixed_ref[...], block, preferred_element_type=jnp.float32
    ).astype(jnp.bfloat16)
    return block


def close(block, half):
    return lax.dot_general(
        block, half, (((0,), (0,)), ((), ())), preferred_element_type=jnp.float32
    )


def one_unit(env_ref, a_ref, w_ref, p, mixed_ref, half_ref, out_ref):
    size = env_ref.shape[-1]
    block = mix_and_multiply(env_ref, a_ref, w_ref, p, mixed_ref, half_ref)
    for v in range(4):
        half = half_ref[v * size : (v + 1) * size, :]
        out_ref[v] = close(block, half).astype(jnp.bfloat16)


def stay_part(env_ref, a_ref, w_ref, mixed_ref, half_ref, mixed2_ref, half2_ref, out_ref):
    size = env_ref.shape[-1]
    first = mix_and_multiply(env_ref, a_ref, w_ref, 1, mixed_ref, half_ref)
    second = mix_and_multiply(env_ref, a_ref, w_ref, 2, mixed2_ref, half2_ref)
    for v in range(4):
        at = slice(v * size, (v + 1) * size)
        total = close(first, half_ref[at, :]) + close(second, half2_ref[at, :])
        out_ref[v] = total.astype(jnp.bfloat16)


def stay_kernel(w_ref, env_ref, a_ref, out_ref, *work):
    stay_part(env_ref, a_ref, w_ref, *work, out_ref)


def moving_parts(p_ref, w_ref, env_ref, a_ref, edge_ref, inner_ref, over_ref, *work):
    edge = p_ref[0]
    one_unit(env_ref, a_ref, w_ref, edge, *work[:2], edge_ref)
    one_unit(env_ref, a_ref, w_ref, 3 - edge, *work[2:], inner_ref)

    @pl.when(p_ref[1] == 1)
    def _():
        stay_part(env_ref, a_ref, w_ref, *work, over_ref)


def first_kernel(p_ref, w_ref, env_ref, a_ref, edge_ref, inner_ref, over_ref, *work):
    moving_parts(p_ref, w_ref, env_ref, a_ref, edge_ref, inner_ref, over_ref, *work)


def summed(turn, cross_ref, swap_ref, came_ref, stay_ref, env_ref):
    size = env_ref.shape[-1]
    step = 32

    def add(one_ref):
        for v in range(4):
            for i in range(0, size, step):
                at = (v, slice(i, i + step))
                total = (
                    swap_ref[at].astype(jnp.float32)
                    + one_ref[at].astype(jnp.float32)
                    + cross_ref[at].astype(jnp.float32)
                )
                env_ref[at] = total.astype(jnp.bfloat16)

    @pl.when(turn == 1)
    def _():
        add(came_ref)

    @pl.when(turn == 0)
    def _():
        add(stay_ref)


def lead_kernel(
    p_ref, w_ref, cross_ref, swap_ref, came_ref, stay_ref, a_ref, env_ref, edge_ref, inner_ref, over_ref, *work
):
    summed(p_ref[2], cross_ref, swap_ref, came_ref, stay_ref, env_ref)
    moving_parts(p_ref, w_ref, env_ref, a_ref, edge_ref, inner_ref, over_ref, *work)


def last_kernel(count, p_ref, cross_ref, swap_ref, came_ref, stay_ref, *refs):
    out_ref, sem = refs[count], refs[count + 1]

    @pl.when(p_ref[0] == 0)
    def _():
        summed(p_ref[1], cross_ref, swap_ref, came_ref, stay_ref, out_ref)

    for i in range(count):

        @pl.when(p_ref[0] == i + 1)
        def _():
            copy = pltpu.make_async_copy(refs[i], out_ref, sem)
            copy.start()
            copy.wait()


def pick_kernel(count, p_ref, *refs):
    out_ref, sem = refs[count], refs[count + 1]
    for i in range(count):

        @pl.when(p_ref[0] == i)
        def _():
            copy = pltpu.make_async_copy(refs[i], out_ref, sem)
            copy.start()
            copy.wait()


VMEM = pl.BlockSpec(memory_space=pltpu.VMEM)
SMEM = pl.BlockSpec(memory_space=pltpu.SMEM)
ANY = pl.BlockSpec(memory_space=pl.ANY)
PARAMS = pltpu.CompilerParams(vmem_limit_bytes=24 * 1024 * 1024)


def scratch(count, channels, size):
    return [pltpu.VMEM((channels * size, size), jnp.bfloat16)] * count


def cost(units, arrays):
    return pl.CostEstimate(
        flops=units * 8 * 2 * 256**3, bytes_accessed=arrays * 2**19, transcendentals=0
    )


def local(site_blocks, operators, op_mask, coupling, start_env):
    sites = lax.axis_size("site")
    sectors = lax.axis_size("sector")
    lines = sectors // RING
    row = lax.axis_index("site")
    place = lax.axis_index("sector")
    slot = lax.rem(place, RING)
    odd = lax.rem(place, 2)
    states, size = site_blocks.shape[2], site_blocks.shape[3]
    block_shape = jax.ShapeDtypeStruct(start_env.shape[1:], jnp.bfloat16)
    channels = start_env.shape[1]

    def at(line, slot_at):
        return line * RING + slot_at % RING

    lane = [(line, u) for line in range(lines) for u in range(RING)]
    coupled = coupling[0, 0].astype(jnp.float32)
    weights = operators[0] * op_mask[0].astype(jnp.float32) * coupled[None, None, :]
    weights = weights.transpose(2, 1, 0).reshape(-1)
    blocks = site_blocks[0, 0].reshape(states * size, size)

    def turn_of(s):
        return (lax.rem(slot + s, RING) == RING - 1).astype(jnp.int32)

    def straight_pairs(s):
        return [((s, at(z, u)), (0, at(z, u - s))) for z, u in lane]

    early = min(3, sites)
    parcels = {s: moved(blocks, straight_pairs(s), sectors) for s in range(1, early)}
    scales = {s: moved(weights, straight_pairs(s), sectors) for s in range(1, early)}
    parcels[0], scales[0] = blocks, weights

    def pack(after):
        held, lying, after = lax.optimization_barrier((weights, blocks, after))
        high = lax.reduce_precision(held, *ROUND)
        middle = lax.reduce_precision(held - high, *ROUND)
        low = lax.reduce_precision(held - high - middle, *ROUND)
        pieces = jnp.stack([high, middle, low]).astype(jnp.bfloat16)
        pieces = jnp.pad(pieces, ((0, 13), (0, size - pieces.shape[1])))
        packed = jnp.concatenate([lying, pieces], axis=0)
        pairs = [((s, at(z, u)), (s, at(z, u - s))) for s in range(early, sites) for z, u in lane]
        return moved(packed, pairs, sectors), after

    def weights_of(parcel):
        parts = parcel[states * size : states * size + 3, : weights.shape[0]].astype(jnp.float32)
        return parts[0] + parts[1] + parts[2]

    def fetch(s, after):
        held, after = lax.optimization_barrier((turned, after))
        pairs = [((s, q), (0, q)) for q in range(sectors)]
        return moved(held, pairs, sectors), after

    def part_pairs(s, crossing):
        pairs = []
        for z, v in lane:
            u = (v + s) % RING
            if (v % 2 == 0) == crossing:
                pairs.append(((0, at(z, v)), (0, at(z, v - 1))))
            elif z + (u >= RING - 2) < lines:
                pairs.append(((0, at(z, v)), (0, at(z + (u >= RING - 2), v + 1))))
        return pairs

    def over_pairs(s):
        v = (RING - 1 - s) % RING
        return [((0, at(z, v)), (0, at(z + 1, v))) for z in range(lines - 1)]

    current = start_env[0]
    kept, raised = {}, {}
    near = min(6, sites)
    work = scratch(4, channels, size)
    for s in range(sites):
        control = jnp.stack([3 * odd, turn_of(s), turn_of(s - 1 + RING)])
        if s == 0:
            edge, inner, over = pl.pallas_call(
                first_kernel,
                out_shape=(block_shape,) * 3,
                in_specs=[SMEM, SMEM, VMEM, VMEM],
                out_specs=(VMEM,) * 3,
                scratch_shapes=work,
                compiler_params=PARAMS,
                cost_estimate=cost(2, 4),
                name="first",
            )(control, scales[0], current, blocks)
        else:
            if s not in scales:
                scales[s] = weights_of(parcels[s])
            current, edge, inner, over = pl.pallas_call(
                lead_kernel,
                out_shape=(block_shape,) * 4,
                in_specs=[SMEM, SMEM] + [VMEM] * 5,
                out_specs=(VMEM,) * 4,
                scratch_shapes=work,
                compiler_params=PARAMS,
                cost_estimate=cost(2, 6),
                name="lead",
            )(control, scales[s], cross, swap, came, stay, parcels[s])
            kept[s] = current
        cross = moved(edge, part_pairs(s, True), sectors)
        swap = moved(inner, part_pairs(s, False), sectors)
        if s == 0:
            turned, swap = pack(swap)
        came = moved(over, over_pairs(s), sectors)
        stay = pl.pallas_call(
            stay_kernel,
            out_shape=block_shape,
            in_specs=[SMEM, VMEM, VMEM],
            out_specs=VMEM,
            scratch_shapes=work,
            compiler_params=PARAMS,
            cost_estimate=cost(40, 4),
            name="stay",
        )(scales[s], current, parcels[s])
        if s >= 1:
            if s < near:
                raised[s] = moved(kept[s], [((0, q), (s, q)) for q in range(sectors)], sectors)
            else:
                raised[s] = moved(
                    kept[s], [((0, at(z, u - s)), (s, at(z, u))) for z, u in lane], sectors
                )
        if s >= 2 and s + 1 < sites:
            stay, raised[s - 1] = lax.optimization_barrier((stay, raised[s - 1]))
        ahead = s + 2
        if early <= ahead < sites:
            parcels[ahead], stay = fetch(ahead, stay)

    picked = pl.pallas_call(
        functools.partial(pick_kernel, near - 1),
        out_shape=block_shape,
        in_specs=[SMEM] + [ANY] * (near - 1),
        out_specs=ANY,
        scratch_shapes=[pltpu.SemaphoreType.DMA],
        name="pick",
    )(jnp.stack([row - 1]), *[raised[r] for r in range(1, near)])
    homeward = moved(
        picked,
        [((r, at(z, u - r)), (r, at(z, u))) for r in range(1, near) for z, u in lane],
        sectors,
    )
    kind = jnp.where(row == 0, 0, jnp.where(row < near, 1, row - near + 2))
    straight = [raised[r] for r in range(near, sites)]
    out = pl.pallas_call(
        functools.partial(last_kernel, 1 + len(straight)),
        out_shape=block_shape,
        in_specs=[SMEM] + [VMEM] * 4 + [ANY] * (1 + len(straight)),
        out_specs=VMEM,
        scratch_shapes=[pltpu.SemaphoreType.DMA],
        compiler_params=PARAMS,
        name="last",
    )(jnp.stack([kind, turn_of(sites - 1)]), cross, swap, came, stay, homeward, *straight)
    return out[None, None]


def solution(mesh):
    return jax.shard_map(
        local,
        mesh=mesh,
        in_specs=(
            P("site", "sector", None, None, None),
            P("site", None, None, None),
            P("site", None, None, None),
            P("site", "sector", None),
            P("sector", None, None, None),
        ),
        out_specs=P("site", "sector", None, None, None),
        check_vma=False,
    )
```

```python
import functools

import jax
import jax.numpy as jnp
from jax import lax
from jax.experimental import pallas as pl
from jax.experimental.pallas import tpu as pltpu
from jax.sharding import PartitionSpec as P

AXES = ("site", "sector")
RING = 8
ROUND = (8, 7)


def moved(x, pairs, sectors):
    flat = [(a * sectors + b, c * sectors + d) for (a, b), (c, d) in pairs]
    return lax.ppermute(x, AXES, flat)


def mix_and_multiply(env_ref, a_ref, w_ref, p, mixed_ref, half_ref):
    size = env_ref.shape[-1]
    step = 32
    for i in range(0, size, step):
        rows = [env_ref[w, i : i + step, :].astype(jnp.float32) for w in range(4)]
        for v in range(4):
            total = rows[0] * w_ref[p * 16 + v * 4]
            for w in range(1, 4):
                total = total + rows[w] * w_ref[p * 16 + v * 4 + w]
            mixed_ref[v * size + i : v * size + i + step, :] = total.astype(jnp.bfloat16)
    block = a_ref[pl.ds(pl.multiple_of(p * size, size), size), :]
    half_ref[...] = jnp.dot(
        mixed_ref[...], block, preferred_element_type=jnp.float32
    ).astype(jnp.bfloat16)
    return block


def close(block, half):
    return lax.dot_general(
        block, half, (((0,), (0,)), ((), ())), preferred_element_type=jnp.float32
    )


def one_unit(env_ref, a_ref, w_ref, p, mixed_ref, half_ref, out_ref):
    size = env_ref.shape[-1]
    block = mix_and_multiply(env_ref, a_ref, w_ref, p, mixed_ref, half_ref)
    for v in range(4):
        half = half_ref[v * size : (v + 1) * size, :]
        out_ref[v] = close(block, half).astype(jnp.bfloat16)


def stay_part(env_ref, a_ref, w_ref, mixed_ref, half_ref, mixed2_ref, half2_ref, out_ref):
    size = env_ref.shape[-1]
    first = mix_and_multiply(env_ref, a_ref, w_ref, 1, mixed_ref, half_ref)
    second = mix_and_multiply(env_ref, a_ref, w_ref, 2, mixed2_ref, half2_ref)
    for v in range(4):
        at = slice(v * size, (v + 1) * size)
        total = close(first, half_ref[at, :]) + close(second, half2_ref[at, :])
        out_ref[v] = total.astype(jnp.bfloat16)


def stay_kernel(w_ref, env_ref, a_ref, out_ref, *work):
    stay_part(env_ref, a_ref, w_ref, *work, out_ref)


def moving_parts(p_ref, w_ref, env_ref, a_ref, edge_ref, inner_ref, *work):
    edge = p_ref[0]
    one_unit(env_ref, a_ref, w_ref, edge, *work[:2], edge_ref)
    one_unit(env_ref, a_ref, w_ref, 3 - edge, *work[2:], inner_ref)


def summed(fresh, cross_ref, swap_ref, stay_ref, env_ref):
    size = env_ref.shape[-1]
    step = 32

    def add(refs):
        for v in range(4):
            for i in range(0, size, step):
                at = (v, slice(i, i + step))
                total = refs[0][at].astype(jnp.float32)
                for ref in refs[1:]:
                    total = total + ref[at].astype(jnp.float32)
                env_ref[at] = total.astype(jnp.bfloat16)

    @pl.when(fresh == 1)
    def _():
        add((swap_ref, cross_ref))

    @pl.when(fresh == 0)
    def _():
        add((swap_ref, stay_ref, cross_ref))


def lead_kernel(
    p_ref, w_ref, cross_ref, swap_ref, stay_ref, a_ref, env_ref, edge_ref, inner_ref, *work
):
    summed(p_ref[1], cross_ref, swap_ref, stay_ref, env_ref)
    moving_parts(p_ref, w_ref, env_ref, a_ref, edge_ref, inner_ref, *work)


def last_kernel(count, p_ref, cross_ref, swap_ref, stay_ref, *refs):
    out_ref, sem = refs[count], refs[count + 1]

    @pl.when(p_ref[0] == 0)
    def _():
        summed(p_ref[1], cross_ref, swap_ref, stay_ref, out_ref)

    for i in range(count):

        @pl.when(p_ref[0] == i + 1)
        def _():
            copy = pltpu.make_async_copy(refs[i], out_ref, sem)
            copy.start()
            copy.wait()


def pick_kernel(count, p_ref, *refs):
    out_ref, sem = refs[count], refs[count + 1]
    for i in range(count):

        @pl.when(p_ref[0] == i)
        def _():
            copy = pltpu.make_async_copy(refs[i], out_ref, sem)
            copy.start()
            copy.wait()


VMEM = pl.BlockSpec(memory_space=pltpu.VMEM)
SMEM = pl.BlockSpec(memory_space=pltpu.SMEM)
ANY = pl.BlockSpec(memory_space=pl.ANY)
PARAMS = pltpu.CompilerParams(vmem_limit_bytes=24 * 1024 * 1024)


def scratch(count, channels, size):
    return [pltpu.VMEM((channels * size, size), jnp.bfloat16)] * count


def cost(units, arrays):
    return pl.CostEstimate(
        flops=units * 8 * 2 * 256**3, bytes_accessed=arrays * 2**19, transcendentals=0
    )


def local(site_blocks, operators, op_mask, coupling, start_env):
    sites = lax.axis_size("site")
    sectors = lax.axis_size("sector")
    row = lax.axis_index("site")
    place = lax.axis_index("sector")
    odd = lax.rem(place, 2)
    states, size = site_blocks.shape[2], site_blocks.shape[3]
    block_shape = jax.ShapeDtypeStruct(start_env.shape[1:], jnp.bfloat16)
    channels = start_env.shape[1]

    def device(position):
        return (0, position) if position >= 0 else (1, position + sites)

    def fresh_of(s):
        position = jnp.where(row == 1, place - sites, place)
        return (position + s < 0).astype(jnp.int32)

    coupled = coupling[0, 0].astype(jnp.float32)
    weights = operators[0] * op_mask[0].astype(jnp.float32) * coupled[None, None, :]
    weights = weights.transpose(2, 1, 0).reshape(-1)
    blocks = site_blocks[0, 0].reshape(states * size, size)

    def straight_pairs(s):
        return [((s, t), device(t - s)) for t in range(sectors)]

    early = min(3, sites)
    parcels = {s: moved(blocks, straight_pairs(s), sectors) for s in range(1, early)}
    scales = {s: moved(weights, straight_pairs(s), sectors) for s in range(1, early)}
    parcels[0], scales[0] = blocks, weights

    def pack(after):
        held, lying, after = lax.optimization_barrier((weights, blocks, after))
        high = lax.reduce_precision(held, *ROUND)
        middle = lax.reduce_precision(held - high, *ROUND)
        low = lax.reduce_precision(held - high - middle, *ROUND)
        pieces = jnp.stack([high, middle, low]).astype(jnp.bfloat16)
        pieces = jnp.pad(pieces, ((0, 13), (0, size - pieces.shape[1])))
        packed = jnp.concatenate([lying, pieces], axis=0)
        pairs = [
            ((s, t), (s, (t - s) % sectors)) for s in range(early, sites) for t in range(sectors)
        ]
        return moved(packed, pairs, sectors), after

    def weights_of(parcel):
        parts = parcel[states * size : states * size + 3, : weights.shape[0]].astype(jnp.float32)
        return parts[0] + parts[1] + parts[2]

    def fetch(s, after):
        held, after = lax.optimization_barrier((turned, after))
        pairs = [((s, (t - s) % sectors), device(t - s)) for t in range(sectors)]
        return moved(held, pairs, sectors), after

    def part_pairs(s, crossing):
        pairs = []
        for t in range(sectors):
            at = t - s
            if (at % 2 == 0) == crossing:
                pairs.append((device(at), device(at - 1)))
            elif t + 2 < sectors:
                pairs.append((device(at), device(at + 1)))
        return pairs

    current = start_env[0]
    kept, raised, direct = {}, {}, {}
    work = scratch(4, channels, size)
    late = sites - 1
    for s in range(sites):
        control = jnp.stack([3 * odd, fresh_of(s - 1)])
        if s == 0:
            edge, inner = pl.pallas_call(
                moving_parts,
                out_shape=(block_shape,) * 2,
                in_specs=[SMEM, SMEM, VMEM, VMEM],
                out_specs=(VMEM,) * 2,
                scratch_shapes=work,
                compiler_params=PARAMS,
                cost_estimate=cost(2, 4),
                name="first",
            )(control, scales[0], current, blocks)
        else:
            if s not in scales:
                scales[s] = weights_of(parcels[s])
            current, edge, inner = pl.pallas_call(
                lead_kernel,
                out_shape=(block_shape,) * 3,
                in_specs=[SMEM, SMEM] + [VMEM] * 4,
                out_specs=(VMEM,) * 3,
                scratch_shapes=work,
                compiler_params=PARAMS,
                cost_estimate=cost(2, 6),
                name="lead",
            )(control, scales[s], cross, swap, stay, parcels[s])
            kept[s] = current
        cross = moved(edge, part_pairs(s, True), sectors)
        swap = moved(inner, part_pairs(s, False), sectors)
        if s == 0:
            turned, scales[1] = pack(scales[1])
        stay = pl.pallas_call(
            stay_kernel,
            out_shape=block_shape,
            in_specs=[SMEM, VMEM, VMEM],
            out_specs=VMEM,
            scratch_shapes=work,
            compiler_params=PARAMS,
            cost_estimate=cost(40, 4),
            name="stay",
        )(scales[s], current, parcels[s])
        if s in (1, late):
            direct[s] = moved(kept[s], [(device(t - s), (s, t)) for t in range(sectors)], sectors)
        elif s:
            raised[s] = moved(
                kept[s],
                [(device(t - s), (s, (t - s) % sectors)) for t in range(sectors)],
                sectors,
            )
        if s - 1 in raised and s < late:
            stay, raised[s - 1] = lax.optimization_barrier((stay, raised[s - 1]))
        ahead = s + 2
        if early <= ahead < sites:
            parcels[ahead], stay = fetch(ahead, stay)

    resting = [raised[r] for r in range(2, late)]
    ended = pl.pallas_call(
        functools.partial(last_kernel, len(resting)),
        out_shape=block_shape,
        in_specs=[SMEM] + [VMEM] * 3 + [ANY] * len(resting),
        out_specs=VMEM,
        scratch_shapes=[pltpu.SemaphoreType.DMA],
        compiler_params=PARAMS,
        name="last",
    )(
        jnp.stack([jnp.maximum(row - 1, 0), fresh_of(sites - 1)]),
        cross,
        swap,
        stay,
        *resting,
    )
    pairs = [(device(t - sites), (0, t)) for t in range(sectors)]
    for r in range(2, late):
        pairs += [((r, (t - r) % sectors), (r, t)) for t in range(sectors)]
    home = moved(ended, pairs, sectors)
    out = pl.pallas_call(
        functools.partial(pick_kernel, 3),
        out_shape=block_shape,
        in_specs=[SMEM, VMEM, ANY, ANY],
        out_specs=ANY,
        scratch_shapes=[pltpu.SemaphoreType.DMA],
        name="pick",
    )(
        jnp.stack([jnp.where(row == 1, 1, jnp.where(row == late, 2, 0))]),
        home,
        direct[1],
        direct[late],
    )
    return out[None, None]


def solution(mesh):
    return jax.shard_map(
        local,
        mesh=mesh,
        in_specs=(
            P("site", "sector", None, None, None),
            P("site", None, None, None),
            P("site", None, None, None),
            P("site", "sector", None),
            P("sector", None, None, None),
        ),
        out_specs=P("site", "sector", None, None, None),
        check_vma=False,
    )
```

```python
import functools

import jax
import jax.numpy as jnp
from jax import lax
from jax.experimental import pallas as pl
from jax.experimental.pallas import tpu as pltpu
from jax.sharding import PartitionSpec as P

AXES = ("site", "sector")


def moved(x, pairs, sectors):
    flat = [(a * sectors + b, c * sectors + d) for (a, b), (c, d) in pairs]
    return lax.ppermute(x, AXES, flat)


def mix_and_multiply(env_ref, a_ref, weight, p, mixed_ref, half_ref):
    size = env_ref.shape[-1]
    step = 32
    for i in range(0, size, step):
        rows = [env_ref[w, i : i + step, :].astype(jnp.float32) for w in range(4)]
        for v in range(4):
            total = rows[0] * weight(p, v, 0)
            for w in range(1, 4):
                total = total + rows[w] * weight(p, v, w)
            mixed_ref[v * size + i : v * size + i + step, :] = total.astype(jnp.bfloat16)
    block = a_ref[pl.ds(pl.multiple_of(p * size, size), size), :]
    half_ref[...] = jnp.dot(
        mixed_ref[...], block, preferred_element_type=jnp.float32
    ).astype(jnp.bfloat16)
    return block


def close(block, half):
    return lax.dot_general(
        block, half, (((0,), (0,)), ((), ())), preferred_element_type=jnp.float32
    )


def one_unit(env_ref, a_ref, weight, p, mixed_ref, half_ref, out_ref):
    size = env_ref.shape[-1]
    block = mix_and_multiply(env_ref, a_ref, weight, p, mixed_ref, half_ref)
    for v in range(4):
        half = half_ref[v * size : (v + 1) * size, :]
        out_ref[v] = close(block, half).astype(jnp.bfloat16)


def listed(w_ref):
    return lambda p, v, w: w_ref[p * 16 + v * 4 + w]


def stay_kernel(w_ref, env_ref, a_ref, out_ref, mixed_ref, half_ref, mixed2_ref, half2_ref):
    size = env_ref.shape[-1]
    weight = listed(w_ref)
    first = mix_and_multiply(env_ref, a_ref, weight, 1, mixed_ref, half_ref)
    second = mix_and_multiply(env_ref, a_ref, weight, 2, mixed2_ref, half2_ref)
    for v in range(4):
        at = slice(v * size, (v + 1) * size)
        total = close(first, half_ref[at, :]) + close(second, half2_ref[at, :])
        out_ref[v] = total.astype(jnp.bfloat16)


def inner_kernel(p_ref, w_ref, env_ref, a_ref, out_ref, *work):
    one_unit(env_ref, a_ref, listed(w_ref), 3 - p_ref[0], *work, out_ref)


def first_kernel(
    p_ref, operator_ref, mask_ref, couple_ref, env_any, a_any, edge_ref, env_ref, a_ref, mixed_ref, half_ref, sems
):
    size = env_ref.shape[-1]
    edge = p_ref[0]
    rows = pl.ds(pl.multiple_of(edge * size, size), size)
    copies = [pltpu.make_async_copy(env_any.at[w], env_ref.at[w], sems.at[w]) for w in range(4)]
    copies.append(pltpu.make_async_copy(a_any.at[rows], a_ref.at[rows], sems.at[4]))
    for copy in copies:
        copy.start()
    for copy in copies:
        copy.wait()

    def weight(p, v, w):
        scale = operator_ref[w, v, p] * mask_ref[w, v, p].astype(jnp.float32)
        return scale * couple_ref[p].astype(jnp.float32)

    one_unit(env_ref, a_ref, weight, edge, mixed_ref, half_ref, edge_ref)


def summed(fresh, cross_ref, swap_ref, stay_ref, env_ref):
    size = env_ref.shape[-1]
    step = 32

    def add(refs):
        for v in range(4):
            for i in range(0, size, step):
                at = (v, slice(i, i + step))
                total = refs[0][at].astype(jnp.float32)
                for ref in refs[1:]:
                    total = total + ref[at].astype(jnp.float32)
                env_ref[at] = total.astype(jnp.bfloat16)

    @pl.when(fresh == 1)
    def _():
        add((swap_ref, cross_ref))

    @pl.when(fresh == 0)
    def _():
        add((swap_ref, stay_ref, cross_ref))


def lead_kernel(p_ref, w_ref, cross_ref, swap_ref, stay_ref, a_ref, env_ref, edge_ref, *work):
    summed(p_ref[1], cross_ref, swap_ref, stay_ref, env_ref)
    one_unit(env_ref, a_ref, listed(w_ref), p_ref[0], *work, edge_ref)


def last_kernel(count, p_ref, cross_ref, swap_ref, stay_ref, *refs):
    out_ref, sem = refs[count], refs[count + 1]

    @pl.when(p_ref[0] == 0)
    def _():
        summed(p_ref[1], cross_ref, swap_ref, stay_ref, out_ref)

    for i in range(count):

        @pl.when(p_ref[0] == i + 1)
        def _():
            copy = pltpu.make_async_copy(refs[i], out_ref, sem)
            copy.start()
            copy.wait()


def pick_kernel(count, p_ref, *refs):
    out_ref, sem = refs[count], refs[count + 1]
    for i in range(count):

        @pl.when(p_ref[0] == i)
        def _():
            copy = pltpu.make_async_copy(refs[i], out_ref, sem)
            copy.start()
            copy.wait()


VMEM = pl.BlockSpec(memory_space=pltpu.VMEM)
SMEM = pl.BlockSpec(memory_space=pltpu.SMEM)
ANY = pl.BlockSpec(memory_space=pl.ANY)
HBM = pl.BlockSpec(memory_space=pltpu.HBM)
WHOLE = pltpu.CompilerParams(vmem_limit_bytes=64400 * 1024)
PARAMS = pltpu.CompilerParams(vmem_limit_bytes=24 * 1024 * 1024)


def scratch(count, channels, size):
    return [pltpu.VMEM((channels * size, size), jnp.bfloat16)] * count


def cost(units, arrays):
    return pl.CostEstimate(
        flops=units * 8 * 2 * 256**3, bytes_accessed=arrays * 2**19, transcendentals=0
    )


def local(site_blocks, operators, op_mask, coupling, start_env):
    sites = lax.axis_size("site")
    sectors = lax.axis_size("sector")
    row = lax.axis_index("site")
    place = lax.axis_index("sector")
    odd = lax.rem(place, 2)
    states, size = site_blocks.shape[2], site_blocks.shape[3]
    block_shape = jax.ShapeDtypeStruct(start_env.shape[1:], jnp.bfloat16)
    channels = start_env.shape[1]

    def device(position):
        return (0, position) if position >= 0 else (1, position + sites)

    def fresh_of(s):
        position = jnp.where(row == 1, place - sites, place)
        return (position + s < 0).astype(jnp.int32)

    coupled = coupling[0, 0].astype(jnp.float32)
    weights = operators[0] * op_mask[0].astype(jnp.float32) * coupled[None, None, :]
    weights = weights.transpose(2, 1, 0).reshape(-1)
    blocks = site_blocks[0, 0].reshape(states * size, size)

    def straight_pairs(s):
        return [((s, t), device(t - s)) for t in range(sectors)]

    early = min(2, sites)
    parcels = {s: moved(blocks, straight_pairs(s), sectors) for s in range(1, early)}
    parcels[0], scales = blocks, {0: weights}
    turned = moved(
        blocks,
        [((s, t), (s, (t - s) % sectors)) for s in range(early, sites) for t in range(sectors)],
        sectors,
    )

    def fetch(s, after):
        held, after = lax.optimization_barrier((turned, after))
        pairs = [((s, (t - s) % sectors), device(t - s)) for t in range(sectors)]
        return moved(held, pairs, sectors), after

    def fetch_weights(s, after):
        held, after = lax.optimization_barrier((weights, after))
        return moved(held, straight_pairs(s), sectors), after

    def part_pairs(s, crossing):
        pairs = []
        for t in range(sectors):
            at = t - s
            if (at % 2 == 0) == crossing:
                pairs.append((device(at), device(at - 1)))
            elif t + 2 < sectors:
                pairs.append((device(at), device(at + 1)))
        return pairs

    current = start_env[0]
    kept, raised, direct = {}, {}, {}
    work = scratch(4, channels, size)
    late = sites - 1
    for s in range(sites):
        control = jnp.stack([3 * odd, fresh_of(s - 1)])
        if s == 0:
            edge = pl.pallas_call(
                first_kernel,
                out_shape=block_shape,
                in_specs=[SMEM] * 4 + [HBM] * 2,
                out_specs=VMEM,
                scratch_shapes=[
                    pltpu.VMEM((channels, size, size), jnp.bfloat16),
                    pltpu.VMEM((states * size, size), jnp.bfloat16),
                ]
                + work[:2]
                + [pltpu.SemaphoreType.DMA((5,))],
                compiler_params=WHOLE,
                cost_estimate=cost(1, 4),
                name="first",
            )(control, operators[0], op_mask[0], coupling[0, 0], current, blocks)
        else:
            current, edge = pl.pallas_call(
                lead_kernel,
                out_shape=(block_shape,) * 2,
                in_specs=[SMEM, SMEM] + [VMEM] * 4,
                out_specs=(VMEM,) * 2,
                scratch_shapes=work[:2],
                compiler_params=PARAMS,
                cost_estimate=cost(1, 6),
                name="lead",
            )(control, scales[s], cross, swap, stay, parcels[s])
            kept[s] = current
        cross = moved(edge, part_pairs(s, True), sectors)
        source = current
        if s == 0:
            source, _ = lax.optimization_barrier((current, edge))
        inner = pl.pallas_call(
            inner_kernel,
            out_shape=block_shape,
            in_specs=[SMEM, SMEM, VMEM, VMEM],
            out_specs=VMEM,
            scratch_shapes=work[:2],
            compiler_params=PARAMS,
            cost_estimate=cost(1, 4),
            name="inner",
        )(control, scales[s], source, parcels[s])
        swap = moved(inner, part_pairs(s, False), sectors)
        stay = pl.pallas_call(
            stay_kernel,
            out_shape=block_shape,
            in_specs=[SMEM, VMEM, VMEM],
            out_specs=VMEM,
            scratch_shapes=work,
            compiler_params=PARAMS,
            cost_estimate=cost(40, 4),
            name="stay",
        )(scales[s], source, parcels[s])
        if s in (1, late):
            direct[s] = moved(kept[s], [(device(t - s), (s, t)) for t in range(sectors)], sectors)
        elif s:
            raised[s] = moved(
                kept[s],
                [(device(t - s), (s, (t - s) % sectors)) for t in range(sectors)],
                sectors,
            )
        if s - 1 in raised and s < late:
            stay, raised[s - 1] = lax.optimization_barrier((stay, raised[s - 1]))
        if s == 0:
            scales[1], swap = fetch_weights(1, swap)
        if s + 2 < sites:
            parcels[s + 2], stay = fetch(s + 2, stay)
            scales[s + 2], stay = fetch_weights(s + 2, stay)

    resting = [raised[r] for r in range(2, late)]
    ended = pl.pallas_call(
        functools.partial(last_kernel, len(resting)),
        out_shape=block_shape,
        in_specs=[SMEM] + [VMEM] * 3 + [ANY] * len(resting),
        out_specs=VMEM,
        scratch_shapes=[pltpu.SemaphoreType.DMA],
        compiler_params=PARAMS,
        name="last",
    )(
        jnp.stack([jnp.maximum(row - 1, 0), fresh_of(sites - 1)]),
        cross,
        swap,
        stay,
        *resting,
    )
    pairs = [(device(t - sites), (0, t)) for t in range(sectors)]
    for r in range(2, late):
        pairs += [((r, (t - r) % sectors), (r, t)) for t in range(sectors)]
    home = moved(ended, pairs, sectors)
    out = pl.pallas_call(
        functools.partial(pick_kernel, 3),
        out_shape=block_shape,
        in_specs=[SMEM, VMEM, ANY, ANY],
        out_specs=VMEM,
        scratch_shapes=[pltpu.SemaphoreType.DMA],
        compiler_params=PARAMS,
        name="pick",
    )(
        jnp.stack([jnp.where(row == 1, 1, jnp.where(row == late, 2, 0))]),
        home,
        direct[1],
        direct[late],
    )
    return out[None, None]


def solution(mesh):
    return jax.shard_map(
        local,
        mesh=mesh,
        in_specs=(
            P("site", "sector", None, None, None),
            P("site", None, None, None),
            P("site", None, None, None),
            P("site", "sector", None),
            P("sector", None, None, None),
        ),
        out_specs=P("site", "sector", None, None, None),
        check_vma=False,
    )
```

```python
import functools

import jax
import jax.numpy as jnp
from jax import lax
from jax.experimental import pallas as pl
from jax.experimental.pallas import tpu as pltpu
from jax.sharding import PartitionSpec as P

AXES = ("site", "sector")
ROUND = (8, 7)


def moved(x, pairs, sectors):
    flat = [(a * sectors + b, c * sectors + d) for (a, b), (c, d) in pairs]
    return lax.ppermute(x, AXES, flat)


def mix_and_multiply(env_ref, a_ref, weight, p, mixed_ref, half_ref):
    size = env_ref.shape[-1]
    step = 32
    for i in range(0, size, step):
        rows = [env_ref[w, i : i + step, :].astype(jnp.float32) for w in range(4)]
        for v in range(4):
            total = rows[0] * weight(p, v, 0)
            for w in range(1, 4):
                total = total + rows[w] * weight(p, v, w)
            mixed_ref[v * size + i : v * size + i + step, :] = total.astype(jnp.bfloat16)
    block = a_ref[pl.ds(pl.multiple_of(p * size, size), size), :]
    half_ref[...] = jnp.dot(
        mixed_ref[...], block, preferred_element_type=jnp.float32
    ).astype(jnp.bfloat16)
    return block


def close(block, half):
    return lax.dot_general(
        block, half, (((0,), (0,)), ((), ())), preferred_element_type=jnp.float32
    )


def one_unit(env_ref, a_ref, weight, p, mixed_ref, half_ref, out_ref):
    size = env_ref.shape[-1]
    block = mix_and_multiply(env_ref, a_ref, weight, p, mixed_ref, half_ref)
    for v in range(4):
        half = half_ref[v * size : (v + 1) * size, :]
        out_ref[v] = close(block, half).astype(jnp.bfloat16)


def listed(w_ref):
    return lambda p, v, w: w_ref[p * 16 + v * 4 + w]


def stay_kernel(w_ref, env_ref, a_ref, out_ref, mixed_ref, half_ref, mixed2_ref, half2_ref):
    size = env_ref.shape[-1]
    weight = listed(w_ref)
    first = mix_and_multiply(env_ref, a_ref, weight, 1, mixed_ref, half_ref)
    second = mix_and_multiply(env_ref, a_ref, weight, 2, mixed2_ref, half2_ref)
    for v in range(4):
        at = slice(v * size, (v + 1) * size)
        total = close(first, half_ref[at, :]) + close(second, half2_ref[at, :])
        out_ref[v] = total.astype(jnp.bfloat16)


def moving_parts(edge, weight, env_ref, a_ref, edge_ref, inner_ref, *work):
    one_unit(env_ref, a_ref, weight, edge, *work[:2], edge_ref)
    one_unit(env_ref, a_ref, weight, 3 - edge, *work[2:], inner_ref)


def first_kernel(
    p_ref, operator_ref, mask_ref, couple_ref, env_any, a_any, edge_ref, inner_ref, env_ref, a_ref, sems, *work
):
    size = env_ref.shape[-1]
    copies = [pltpu.make_async_copy(env_any.at[w], env_ref.at[w], sems.at[w]) for w in range(4)]
    for i, p in enumerate((0, 3)):
        rows = pl.ds(p * size, size)
        copies.append(pltpu.make_async_copy(a_any.at[rows], a_ref.at[rows], sems.at[4 + i]))
    for copy in copies:
        copy.start()
    for copy in copies:
        copy.wait()

    def weight(p, v, w):
        scale = operator_ref[w, v, p] * mask_ref[w, v, p].astype(jnp.float32)
        return scale * couple_ref[p].astype(jnp.float32)

    moving_parts(p_ref[0], weight, env_ref, a_ref, edge_ref, inner_ref, *work)


def summed(fresh, cross_ref, swap_ref, stay_ref, env_ref):
    size = env_ref.shape[-1]
    step = 32

    def add(refs):
        for v in range(4):
            for i in range(0, size, step):
                at = (v, slice(i, i + step))
                total = refs[0][at].astype(jnp.float32)
                for ref in refs[1:]:
                    total = total + ref[at].astype(jnp.float32)
                env_ref[at] = total.astype(jnp.bfloat16)

    @pl.when(fresh == 1)
    def _():
        add((swap_ref, cross_ref))

    @pl.when(fresh == 0)
    def _():
        add((swap_ref, stay_ref, cross_ref))


def lead_kernel(
    p_ref, w_ref, cross_ref, swap_ref, stay_ref, a_ref, env_ref, edge_ref, inner_ref, *work
):
    summed(p_ref[1], cross_ref, swap_ref, stay_ref, env_ref)
    moving_parts(p_ref[0], listed(w_ref), env_ref, a_ref, edge_ref, inner_ref, *work)


def last_kernel(p_ref, cross_ref, swap_ref, stay_ref, out_ref):
    summed(p_ref[0], cross_ref, swap_ref, stay_ref, out_ref)


def pick_kernel(count, p_ref, *refs):
    out_ref, sem = refs[count], refs[count + 1]
    for i in range(count):

        @pl.when(p_ref[0] == i)
        def _():
            copy = pltpu.make_async_copy(refs[i], out_ref, sem)
            copy.start()
            copy.wait()


VMEM = pl.BlockSpec(memory_space=pltpu.VMEM)
SMEM = pl.BlockSpec(memory_space=pltpu.SMEM)
ANY = pl.BlockSpec(memory_space=pl.ANY)
HBM = pl.BlockSpec(memory_space=pltpu.HBM)
WHOLE = pltpu.CompilerParams(vmem_limit_bytes=64400 * 1024)
PARAMS = pltpu.CompilerParams(vmem_limit_bytes=24 * 1024 * 1024)


def scratch(count, channels, size):
    return [pltpu.VMEM((channels * size, size), jnp.bfloat16)] * count


def cost(units, arrays):
    return pl.CostEstimate(
        flops=units * 8 * 2 * 256**3, bytes_accessed=arrays * 2**19, transcendentals=0
    )


def local(site_blocks, operators, op_mask, coupling, start_env):
    sites = lax.axis_size("site")
    sectors = lax.axis_size("sector")
    row = lax.axis_index("site")
    place = lax.axis_index("sector")
    odd = lax.rem(place, 2)
    states, size = site_blocks.shape[2], site_blocks.shape[3]
    block_shape = jax.ShapeDtypeStruct(start_env.shape[1:], jnp.bfloat16)
    channels = start_env.shape[1]

    def device(position):
        return (0, position) if position >= 0 else (1, position + sites)

    def fresh_of(s):
        position = jnp.where(row == 1, place - sites, place)
        return (position + s < 0).astype(jnp.int32)

    coupled = coupling[0, 0].astype(jnp.float32)
    weights = operators[0] * op_mask[0].astype(jnp.float32) * coupled[None, None, :]
    weights = weights.transpose(2, 1, 0).reshape(-1)
    blocks = site_blocks[0, 0].reshape(states * size, size)

    def straight_pairs(s):
        return [((s, t), device(t - s)) for t in range(sectors)]

    parcels = {0: blocks, 1: moved(blocks, straight_pairs(1), sectors)}
    scales = {0: weights, 1: moved(weights, straight_pairs(1), sectors)}

    def pack(after):
        held, lying, after = lax.optimization_barrier((weights, blocks, after))
        high = lax.reduce_precision(held, *ROUND)
        middle = lax.reduce_precision(held - high, *ROUND)
        low = lax.reduce_precision(held - high - middle, *ROUND)
        pieces = jnp.stack([high, middle, low]).astype(jnp.bfloat16)
        pieces = jnp.pad(pieces, ((0, 13), (0, size - pieces.shape[1])))
        return jnp.concatenate([lying, pieces], axis=0), after

    def weights_of(parcel):
        parts = parcel[states * size : states * size + 3, : weights.shape[0]].astype(jnp.float32)
        return parts[0] + parts[1] + parts[2]

    def fetch(s, after):
        held, after = lax.optimization_barrier((packed, after))
        return moved(held, straight_pairs(s), sectors), after

    def part_pairs(s, crossing):
        pairs = []
        for t in range(sectors):
            at = t - s
            if (at % 2 == 0) == crossing:
                pairs.append((device(at), device(at - 1)))
            elif t + 2 < sectors:
                pairs.append((device(at), device(at + 1)))
        return pairs

    current = start_env[0]
    homed = {}
    work = scratch(4, channels, size)
    for s in range(sites):
        control = jnp.stack([3 * odd, fresh_of(s - 1)])
        if s == 0:
            edge, inner = pl.pallas_call(
                first_kernel,
                out_shape=(block_shape,) * 2,
                in_specs=[SMEM] * 4 + [HBM] * 2,
                out_specs=(VMEM,) * 2,
                scratch_shapes=[
                    pltpu.VMEM((channels, size, size), jnp.bfloat16),
                    pltpu.VMEM((states * size, size), jnp.bfloat16),
                    pltpu.SemaphoreType.DMA((6,)),
                ]
                + work,
                compiler_params=WHOLE,
                cost_estimate=cost(2, 4),
                name="first",
            )(control, operators[0], op_mask[0], coupling[0, 0], current, blocks)
        else:
            if s > 1:
                scales[s] = weights_of(parcels[s])
            current, edge, inner = pl.pallas_call(
                lead_kernel,
                out_shape=(block_shape,) * 3,
                in_specs=[SMEM, SMEM] + [VMEM] * 4,
                out_specs=(VMEM,) * 3,
                scratch_shapes=work,
                compiler_params=PARAMS,
                cost_estimate=cost(2, 6),
                name="lead",
            )(control, scales[s], cross, swap, stay, parcels[s])
        cross = moved(edge, part_pairs(s, True), sectors)
        source = current
        if s == 0:
            source, _ = lax.optimization_barrier((current, edge))
        swap = moved(inner, part_pairs(s, False), sectors)
        stay = pl.pallas_call(
            stay_kernel,
            out_shape=block_shape,
            in_specs=[SMEM, VMEM, VMEM],
            out_specs=VMEM,
            scratch_shapes=work,
            compiler_params=PARAMS,
            cost_estimate=cost(40, 4),
            name="stay",
        )(scales[s], source, parcels[s])
        if s == 0:
            packed, scales[1] = pack(scales[1])
        else:
            homed[s] = moved(current, [(device(t - s), (s, t)) for t in range(sectors)], sectors)
        if 2 <= s < sites - 1:
            stay, homed[s - 1] = lax.optimization_barrier((stay, homed[s - 1]))
        if s + 2 < sites:
            parcels[s + 2], stay = fetch(s + 2, stay)

    ended = pl.pallas_call(
        last_kernel,
        out_shape=block_shape,
        in_specs=[SMEM] + [VMEM] * 3,
        out_specs=VMEM,
        compiler_params=PARAMS,
        name="last",
    )(fresh_of(sites - 1)[None], cross, swap, stay)
    homed[0] = moved(ended, [(device(t - sites), (0, t)) for t in range(sectors)], sectors)
    out = pl.pallas_call(
        functools.partial(pick_kernel, sites),
        out_shape=block_shape,
        in_specs=[SMEM, VMEM] + [ANY] * (sites - 1),
        out_specs=VMEM,
        scratch_shapes=[pltpu.SemaphoreType.DMA],
        compiler_params=PARAMS,
        name="pick",
    )(row[None], *[homed[r] for r in range(sites)])
    return out[None, None]


def solution(mesh):
    return jax.shard_map(
        local,
        mesh=mesh,
        in_specs=(
            P("site", "sector", None, None, None),
            P("site", None, None, None),
            P("site", None, None, None),
            P("site", "sector", None),
            P("sector", None, None, None),
        ),
        out_specs=P("site", "sector", None, None, None),
        check_vma=False,
    )
```

```python
import functools

import jax
import jax.numpy as jnp
from jax import lax
from jax.experimental import pallas as pl
from jax.experimental.pallas import tpu as pltpu
from jax.sharding import PartitionSpec as P

AXES = ("site", "sector")
ROUND = (8, 7)


def moved(x, pairs, sectors):
    flat = [(a * sectors + b, c * sectors + d) for (a, b), (c, d) in pairs]
    return lax.ppermute(x, AXES, flat)


def mix_and_multiply(env_ref, a_ref, weight, p, mixed_ref, half_ref):
    size = env_ref.shape[-1]
    step = 32
    for i in range(0, size, step):
        rows = [env_ref[w, i : i + step, :].astype(jnp.float32) for w in range(4)]
        for v in range(4):
            total = rows[0] * weight(p, v, 0)
            for w in range(1, 4):
                total = total + rows[w] * weight(p, v, w)
            mixed_ref[v * size + i : v * size + i + step, :] = total.astype(jnp.bfloat16)
    block = a_ref[pl.ds(pl.multiple_of(p * size, size), size), :]
    half_ref[...] = jnp.dot(
        mixed_ref[...], block, preferred_element_type=jnp.float32
    ).astype(jnp.bfloat16)
    return block


def close(block, half):
    return lax.dot_general(
        block, half, (((0,), (0,)), ((), ())), preferred_element_type=jnp.float32
    )


def one_unit(env_ref, a_ref, weight, p, mixed_ref, half_ref, out_ref):
    size = env_ref.shape[-1]
    block = mix_and_multiply(env_ref, a_ref, weight, p, mixed_ref, half_ref)
    for v in range(4):
        half = half_ref[v * size : (v + 1) * size, :]
        out_ref[v] = close(block, half).astype(jnp.bfloat16)


def listed(w_ref):
    return lambda p, v, w: w_ref[p * 16 + v * 4 + w]


def stay_kernel(w_ref, env_ref, a_ref, out_ref, mixed_ref, half_ref, mixed2_ref, half2_ref):
    size = env_ref.shape[-1]
    weight = listed(w_ref)
    first = mix_and_multiply(env_ref, a_ref, weight, 1, mixed_ref, half_ref)
    second = mix_and_multiply(env_ref, a_ref, weight, 2, mixed2_ref, half2_ref)
    for v in range(4):
        at = slice(v * size, (v + 1) * size)
        total = close(first, half_ref[at, :]) + close(second, half2_ref[at, :])
        out_ref[v] = total.astype(jnp.bfloat16)


def moving_parts(edge, weight, env_ref, a_ref, edge_ref, inner_ref, *work):
    one_unit(env_ref, a_ref, weight, edge, *work[:2], edge_ref)
    one_unit(env_ref, a_ref, weight, 3 - edge, *work[2:], inner_ref)


def first_kernel(
    p_ref, operator_ref, mask_ref, couple_ref, env_any, a_any, edge_ref, inner_ref, env_ref, a_ref, sems, *work
):
    size = env_ref.shape[-1]
    copies = [pltpu.make_async_copy(env_any.at[w], env_ref.at[w], sems.at[w]) for w in range(4)]
    for i, p in enumerate((0, 3)):
        rows = pl.ds(p * size, size)
        copies.append(pltpu.make_async_copy(a_any.at[rows], a_ref.at[rows], sems.at[4 + i]))
    for copy in copies:
        copy.start()
    for copy in copies:
        copy.wait()

    def weight(p, v, w):
        scale = operator_ref[w, v, p] * mask_ref[w, v, p].astype(jnp.float32)
        return scale * couple_ref[p].astype(jnp.float32)

    moving_parts(p_ref[0], weight, env_ref, a_ref, edge_ref, inner_ref, *work)


def summed(cross_ref, swap_ref, stay_ref, env_ref):
    size = env_ref.shape[-1]
    step = 32
    for v in range(4):
        for i in range(0, size, step):
            at = (v, slice(i, i + step))
            total = swap_ref[at].astype(jnp.float32) + stay_ref[at].astype(jnp.float32)
            env_ref[at] = (total + cross_ref[at].astype(jnp.float32)).astype(jnp.bfloat16)


def lead_kernel(
    p_ref, w_ref, cross_ref, swap_ref, stay_ref, a_ref, env_ref, edge_ref, inner_ref, *work
):
    summed(cross_ref, swap_ref, stay_ref, env_ref)
    moving_parts(p_ref[0], listed(w_ref), env_ref, a_ref, edge_ref, inner_ref, *work)


def last_kernel(cross_ref, swap_ref, stay_ref, out_ref):
    summed(cross_ref, swap_ref, stay_ref, out_ref)


def pick_kernel(count, p_ref, *refs):
    out_ref, sem = refs[count], refs[count + 1]
    for i in range(count):

        @pl.when(p_ref[0] == i)
        def _():
            copy = pltpu.make_async_copy(refs[i], out_ref, sem)
            copy.start()
            copy.wait()


VMEM = pl.BlockSpec(memory_space=pltpu.VMEM)
SMEM = pl.BlockSpec(memory_space=pltpu.SMEM)
ANY = pl.BlockSpec(memory_space=pl.ANY)
HBM = pl.BlockSpec(memory_space=pltpu.HBM)
WHOLE = pltpu.CompilerParams(vmem_limit_bytes=64400 * 1024)
PARAMS = pltpu.CompilerParams(vmem_limit_bytes=24 * 1024 * 1024)


def scratch(count, channels, size):
    return [pltpu.VMEM((channels * size, size), jnp.bfloat16)] * count


def cost(units, arrays):
    return pl.CostEstimate(
        flops=units * 8 * 2 * 256**3, bytes_accessed=arrays * 2**19, transcendentals=0
    )


def local(site_blocks, operators, op_mask, coupling, start_env):
    sites = lax.axis_size("site")
    sectors = lax.axis_size("sector")
    row = lax.axis_index("site")
    place = lax.axis_index("sector")
    odd = lax.rem(place, 2)
    states, size = site_blocks.shape[2], site_blocks.shape[3]
    block_shape = jax.ShapeDtypeStruct(start_env.shape[1:], jnp.bfloat16)
    channels = start_env.shape[1]

    def device(position):
        return (0, position) if position >= 0 else (1, position + sites)

    coupled = coupling[0, 0].astype(jnp.float32)
    weights = operators[0] * op_mask[0].astype(jnp.float32) * coupled[None, None, :]
    weights = weights.transpose(2, 1, 0).reshape(-1)
    rooted = jnp.where(row == 0, weights, 0.0)
    blocks = site_blocks[0, 0].reshape(states * size, size)

    def straight_pairs(s):
        return [((s, t), device(t - s)) for t in range(sectors)]

    def turn_pairs(s):
        return [((s, t), (s, (t - s) % sectors)) for t in range(sectors)]

    parcels = {0: blocks, 1: moved(blocks, straight_pairs(1), sectors)}
    scales = {0: rooted, 1: moved(weights, straight_pairs(1), sectors)}
    turned = {2: moved(blocks, turn_pairs(2), sectors)}

    def pack(after):
        held, lying, after = lax.optimization_barrier((weights, blocks, after))
        high = lax.reduce_precision(held, *ROUND)
        middle = lax.reduce_precision(held - high, *ROUND)
        low = lax.reduce_precision(held - high - middle, *ROUND)
        pieces = jnp.stack([high, middle, low]).astype(jnp.bfloat16)
        pieces = jnp.pad(pieces, ((0, 13), (0, size - pieces.shape[1])))
        return jnp.concatenate([lying, pieces], axis=0), after

    def weights_of(parcel):
        parts = parcel[states * size : states * size + 3, : weights.shape[0]].astype(jnp.float32)
        return parts[0] + parts[1] + parts[2]

    def fetch(s, after):
        held, after = lax.optimization_barrier((turned[s], after))
        pairs = [((s, (t - s) % sectors), device(t - s)) for t in range(sectors)]
        return moved(held, pairs, sectors), after

    def part_pairs(crossing):
        pairs = []
        for at in range(-sites, sectors):
            to = at - 1 if (at % 2 == 0) == crossing else at + 1
            if -sites <= to < sectors:
                pairs.append((device(at), device(to)))
        return pairs

    control = jnp.stack([3 * odd])
    began = jnp.where(row == 0, coupling[0, 0], 0)
    current = start_env[0]
    homed, raised = {}, {}
    work = scratch(4, channels, size)
    for s in range(sites):
        if s == 0:
            edge, inner = pl.pallas_call(
                first_kernel,
                out_shape=(block_shape,) * 2,
                in_specs=[SMEM] * 4 + [HBM] * 2,
                out_specs=(VMEM,) * 2,
                scratch_shapes=[
                    pltpu.VMEM((channels, size, size), jnp.bfloat16),
                    pltpu.VMEM((states * size, size), jnp.bfloat16),
                    pltpu.SemaphoreType.DMA((6,)),
                ]
                + work,
                compiler_params=WHOLE,
                cost_estimate=cost(2, 4),
                name="first",
            )(control, operators[0], op_mask[0], began, current, blocks)
        else:
            if s not in scales:
                scales[s] = weights_of(parcels[s])
            current, edge, inner = pl.pallas_call(
                lead_kernel,
                out_shape=(block_shape,) * 3,
                in_specs=[SMEM, SMEM] + [VMEM] * 4,
                out_specs=(VMEM,) * 3,
                scratch_shapes=work,
                compiler_params=PARAMS,
                cost_estimate=cost(2, 6),
                name="lead",
            )(control, scales[s], cross, swap, stay, parcels[s])
        cross = moved(edge, part_pairs(True), sectors)
        source = current
        if s == 0:
            source, _ = lax.optimization_barrier((current, edge))
        swap = moved(inner, part_pairs(False), sectors)
        stay = pl.pallas_call(
            stay_kernel,
            out_shape=block_shape,
            in_specs=[SMEM, VMEM, VMEM],
            out_specs=VMEM,
            scratch_shapes=work,
            compiler_params=PARAMS,
            cost_estimate=cost(40, 4),
            name="stay",
        )(scales[s], source, parcels[s])
        if s == 0:
            packed, scales[1] = pack(scales[1])
            for r in range(3, sites):
                turned[r] = moved(packed, turn_pairs(r), sectors)
            scales[2] = moved(weights, straight_pairs(2), sectors)
        elif s < sites - 2:
            pairs = [(device(t - s), (s, (t - s) % sectors)) for t in range(sectors)]
            raised[s] = moved(current, pairs, sectors)
        else:
            homed[s] = moved(current, [(device(t - s), (s, t)) for t in range(sectors)], sectors)
        if s - 2 in homed and s < sites - 1:
            stay, homed[s - 2] = lax.optimization_barrier((stay, homed[s - 2]))
        if s - 1 in raised:
            stay, risen = lax.optimization_barrier((stay, raised[s - 1]))
            pairs = [((s - 1, (t - s + 1) % sectors), (s - 1, t)) for t in range(sectors)]
            homed[s - 1] = moved(risen, pairs, sectors)
        if s + 2 < sites:
            parcels[s + 2], stay = fetch(s + 2, stay)

    ended = pl.pallas_call(
        last_kernel,
        out_shape=block_shape,
        in_specs=[VMEM] * 3,
        out_specs=VMEM,
        compiler_params=PARAMS,
        name="last",
    )(cross, swap, stay)
    homed[0] = moved(ended, [(device(t - sites), (0, t)) for t in range(sectors)], sectors)
    out = pl.pallas_call(
        functools.partial(pick_kernel, sites),
        out_shape=block_shape,
        in_specs=[SMEM, VMEM] + [ANY] * (sites - 1),
        out_specs=VMEM,
        scratch_shapes=[pltpu.SemaphoreType.DMA],
        compiler_params=PARAMS,
        name="pick",
    )(row[None], *[homed[r] for r in range(sites)])
    return out[None, None]


def solution(mesh):
    return jax.shard_map(
        local,
        mesh=mesh,
        in_specs=(
            P("site", "sector", None, None, None),
            P("site", None, None, None),
            P("site", None, None, None),
            P("site", "sector", None),
            P("sector", None, None, None),
        ),
        out_specs=P("site", "sector", None, None, None),
        check_vma=False,
    )
```

```python
import functools

import jax
import jax.numpy as jnp
from jax import lax
from jax.experimental import pallas as pl
from jax.experimental.pallas import tpu as pltpu
from jax.sharding import PartitionSpec as P

AXES = ("site", "sector")
ROUND = (8, 7)


def moved(x, pairs, sectors):
    flat = [(a * sectors + b, c * sectors + d) for (a, b), (c, d) in pairs]
    return lax.ppermute(x, AXES, flat)


def mix_and_multiply(env_ref, a_ref, weight, p, mixed_ref, half_ref):
    size = env_ref.shape[-1]
    step = 32
    for i in range(0, size, step):
        rows = [env_ref[w, i : i + step, :].astype(jnp.float32) for w in range(4)]
        for v in range(4):
            total = rows[0] * weight(p, v, 0)
            for w in range(1, 4):
                total = total + rows[w] * weight(p, v, w)
            mixed_ref[v * size + i : v * size + i + step, :] = total.astype(jnp.bfloat16)
    block = a_ref[pl.ds(pl.multiple_of(p * size, size), size), :]
    half_ref[...] = jnp.dot(
        mixed_ref[...], block, preferred_element_type=jnp.float32
    ).astype(jnp.bfloat16)
    return block


def close(block, half):
    return lax.dot_general(
        block, half, (((0,), (0,)), ((), ())), preferred_element_type=jnp.float32
    )


def one_unit(env_ref, a_ref, weight, p, mixed_ref, half_ref, out_ref):
    size = env_ref.shape[-1]
    block = mix_and_multiply(env_ref, a_ref, weight, p, mixed_ref, half_ref)
    for v in range(4):
        half = half_ref[v * size : (v + 1) * size, :]
        out_ref[v] = close(block, half).astype(jnp.bfloat16)


def listed(w_ref):
    return lambda p, v, w: w_ref[p * 16 + v * 4 + w]


def stay_kernel(w_ref, env_ref, a_ref, out_ref, mixed_ref, half_ref, mixed2_ref, half2_ref):
    size = env_ref.shape[-1]
    weight = listed(w_ref)
    first = mix_and_multiply(env_ref, a_ref, weight, 1, mixed_ref, half_ref)
    second = mix_and_multiply(env_ref, a_ref, weight, 2, mixed2_ref, half2_ref)
    for v in range(4):
        at = slice(v * size, (v + 1) * size)
        total = close(first, half_ref[at, :]) + close(second, half2_ref[at, :])
        out_ref[v] = total.astype(jnp.bfloat16)


def moving_parts(edge, weight, env_ref, a_ref, edge_ref, inner_ref, *work):
    one_unit(env_ref, a_ref, weight, edge, *work[:2], edge_ref)
    one_unit(env_ref, a_ref, weight, 3 - edge, *work[2:], inner_ref)


def first_kernel(
    p_ref, operator_ref, mask_ref, couple_ref, env_any, a_any, edge_ref, inner_ref, env_ref, a_ref, sems, *work
):
    size = env_ref.shape[-1]
    copies = [pltpu.make_async_copy(env_any.at[w], env_ref.at[w], sems.at[w]) for w in range(4)]
    for i, p in enumerate((0, 3)):
        rows = pl.ds(p * size, size)
        copies.append(pltpu.make_async_copy(a_any.at[rows], a_ref.at[rows], sems.at[4 + i]))
    for copy in copies:
        copy.start()
    for copy in copies:
        copy.wait()

    def weight(p, v, w):
        scale = operator_ref[w, v, p] * mask_ref[w, v, p].astype(jnp.float32)
        return scale * couple_ref[p].astype(jnp.float32)

    moving_parts(p_ref[0], weight, env_ref, a_ref, edge_ref, inner_ref, *work)


def summed(cross_ref, swap_ref, stay_ref, env_ref):
    size = env_ref.shape[-1]
    step = 32
    for v in range(4):
        for i in range(0, size, step):
            at = (v, slice(i, i + step))
            total = swap_ref[at].astype(jnp.float32) + stay_ref[at].astype(jnp.float32)
            env_ref[at] = (total + cross_ref[at].astype(jnp.float32)).astype(jnp.bfloat16)


def lead_kernel(
    p_ref, w_ref, cross_ref, swap_ref, stay_ref, a_ref, env_ref, edge_ref, inner_ref, *work
):
    summed(cross_ref, swap_ref, stay_ref, env_ref)
    moving_parts(p_ref[0], listed(w_ref), env_ref, a_ref, edge_ref, inner_ref, *work)


def last_kernel(cross_ref, swap_ref, stay_ref, out_ref):
    summed(cross_ref, swap_ref, stay_ref, out_ref)


def pick_kernel(count, p_ref, *refs):
    out_ref, sem = refs[count], refs[count + 1]
    for i in range(count):

        @pl.when(p_ref[0] == i)
        def _():
            copy = pltpu.make_async_copy(refs[i], out_ref, sem)
            copy.start()
            copy.wait()


VMEM = pl.BlockSpec(memory_space=pltpu.VMEM)
SMEM = pl.BlockSpec(memory_space=pltpu.SMEM)
ANY = pl.BlockSpec(memory_space=pl.ANY)
HBM = pl.BlockSpec(memory_space=pltpu.HBM)
WHOLE = pltpu.CompilerParams(vmem_limit_bytes=64400 * 1024)
PARAMS = pltpu.CompilerParams(vmem_limit_bytes=24 * 1024 * 1024)


def scratch(count, channels, size):
    return [pltpu.VMEM((channels * size, size), jnp.bfloat16)] * count


def cost(units, arrays):
    return pl.CostEstimate(
        flops=units * 8 * 2 * 256**3, bytes_accessed=arrays * 2**19, transcendentals=0
    )


def local(site_blocks, operators, op_mask, coupling, start_env):
    sites = lax.axis_size("site")
    sectors = lax.axis_size("sector")
    row = lax.axis_index("site")
    place = lax.axis_index("sector")
    odd = lax.rem(place, 2)
    states, size = site_blocks.shape[2], site_blocks.shape[3]
    block_shape = jax.ShapeDtypeStruct(start_env.shape[1:], jnp.bfloat16)
    channels = start_env.shape[1]

    def device(position):
        return (0, position) if position >= 0 else (1, position + sites)

    coupled = coupling[0, 0].astype(jnp.float32)
    weights = operators[0] * op_mask[0].astype(jnp.float32) * coupled[None, None, :]
    weights = weights.transpose(2, 1, 0).reshape(-1)
    rooted = jnp.where(row == 0, weights, 0.0)
    blocks = site_blocks[0, 0].reshape(states * size, size)

    def straight_pairs(s):
        return [((s, t), device(t - s)) for t in range(sectors)]

    def turn_pairs(s):
        return [((s, t), (s, (t - s) % sectors)) for t in range(sectors)]

    parcels = {0: blocks, 1: moved(blocks, straight_pairs(1), sectors)}
    scales = {0: rooted, 1: moved(weights, straight_pairs(1), sectors)}
    turned = {}

    def pack(after):
        held, lying, after = lax.optimization_barrier((weights, blocks, after))
        high = lax.reduce_precision(held, *ROUND)
        middle = lax.reduce_precision(held - high, *ROUND)
        low = lax.reduce_precision(held - high - middle, *ROUND)
        pieces = jnp.stack([high, middle, low]).astype(jnp.bfloat16)
        pieces = jnp.pad(pieces, ((0, 13), (0, size - pieces.shape[1])))
        return jnp.concatenate([lying, pieces], axis=0), after

    def weights_of(parcel):
        parts = parcel[states * size : states * size + 3, : weights.shape[0]].astype(jnp.float32)
        return parts[0] + parts[1] + parts[2]

    def fetch(s, after):
        if s not in turned:
            held, after = lax.optimization_barrier((blocks, after))
            return moved(held, straight_pairs(s), sectors), after
        held, after = lax.optimization_barrier((turned[s], after))
        pairs = [((s, (t - s) % sectors), device(t - s)) for t in range(sectors)]
        return moved(held, pairs, sectors), after

    def part_pairs(crossing):
        pairs = []
        for at in range(-sites, sectors):
            to = at - 1 if (at % 2 == 0) == crossing else at + 1
            if -sites <= to < sectors:
                pairs.append((device(at), device(to)))
        return pairs

    control = jnp.stack([3 * odd])
    began = jnp.where(row == 0, coupling[0, 0], 0)
    current = start_env[0]
    homed, raised = {}, {}
    work = scratch(4, channels, size)
    for s in range(sites):
        if s == 0:
            edge, inner = pl.pallas_call(
                first_kernel,
                out_shape=(block_shape,) * 2,
                in_specs=[SMEM] * 4 + [HBM] * 2,
                out_specs=(VMEM,) * 2,
                scratch_shapes=[
                    pltpu.VMEM((channels, size, size), jnp.bfloat16),
                    pltpu.VMEM((states * size, size), jnp.bfloat16),
                    pltpu.SemaphoreType.DMA((6,)),
                ]
                + work,
                compiler_params=WHOLE,
                cost_estimate=cost(2, 4),
                name="first",
            )(control, operators[0], op_mask[0], began, current, blocks)
        else:
            if s not in scales:
                scales[s] = weights_of(parcels[s])
            current, edge, inner = pl.pallas_call(
                lead_kernel,
                out_shape=(block_shape,) * 3,
                in_specs=[SMEM, SMEM] + [VMEM] * 4,
                out_specs=(VMEM,) * 3,
                scratch_shapes=work,
                compiler_params=PARAMS,
                cost_estimate=cost(2, 6),
                name="lead",
            )(control, scales[s], cross, swap, stay, parcels[s])
        cross = moved(edge, part_pairs(True), sectors)
        source = current
        if s == 0:
            source, _ = lax.optimization_barrier((current, edge))
        swap = moved(inner, part_pairs(False), sectors)
        stay = pl.pallas_call(
            stay_kernel,
            out_shape=block_shape,
            in_specs=[SMEM, VMEM, VMEM],
            out_specs=VMEM,
            scratch_shapes=work,
            compiler_params=PARAMS,
            cost_estimate=cost(10, 4),
            name="stay",
        )(scales[s], source, parcels[s])
        if s == 0:
            packed, swap = pack(swap)
            for r in range(3, sites):
                turned[r] = moved(packed, turn_pairs(r), sectors)
            scales[2] = moved(weights, straight_pairs(2), sectors)
        elif s < sites - 2:
            pairs = [(device(t - s), (s, (t - s) % sectors)) for t in range(sectors)]
            raised[s] = moved(current, pairs, sectors)
        else:
            homed[s] = moved(current, [(device(t - s), (s, t)) for t in range(sectors)], sectors)
        if s - 2 in homed and s < sites - 1:
            stay, homed[s - 2] = lax.optimization_barrier((stay, homed[s - 2]))
        if s - 1 in raised:
            stay, risen = lax.optimization_barrier((stay, raised[s - 1]))
            pairs = [((s - 1, (t - s + 1) % sectors), (s - 1, t)) for t in range(sectors)]
            homed[s - 1] = moved(risen, pairs, sectors)
        for ahead in (2, 3) if s == 0 else (s + 3,):
            if ahead < sites:
                parcels[ahead], stay = fetch(ahead, stay)

    ended = pl.pallas_call(
        last_kernel,
        out_shape=block_shape,
        in_specs=[VMEM] * 3,
        out_specs=VMEM,
        compiler_params=PARAMS,
        name="last",
    )(cross, swap, stay)
    homed[0] = moved(ended, [(device(t - sites), (0, t)) for t in range(sectors)], sectors)
    out = pl.pallas_call(
        functools.partial(pick_kernel, sites),
        out_shape=block_shape,
        in_specs=[SMEM, VMEM] + [ANY] * (sites - 1),
        out_specs=VMEM,
        scratch_shapes=[pltpu.SemaphoreType.DMA],
        compiler_params=PARAMS,
        name="pick",
    )(row[None], *[homed[r] for r in range(sites)])
    return out[None, None]


def solution(mesh):
    return jax.shard_map(
        local,
        mesh=mesh,
        in_specs=(
            P("site", "sector", None, None, None),
            P("site", None, None, None),
            P("site", None, None, None),
            P("site", "sector", None),
            P("sector", None, None, None),
        ),
        out_specs=P("site", "sector", None, None, None),
        check_vma=False,
    )
```

```python
import functools

import jax
import jax.numpy as jnp
from jax import lax
from jax.experimental import pallas as pl
from jax.experimental.pallas import tpu as pltpu
from jax.sharding import PartitionSpec as P

AXES = ("site", "sector")
ROUND = (8, 7)


def moved(x, pairs, sectors):
    flat = [(a * sectors + b, c * sectors + d) for (a, b), (c, d) in pairs]
    return lax.ppermute(x, AXES, flat)


def mix_and_multiply(env_ref, a_ref, weight, p, mixed_ref, half_ref):
    size = env_ref.shape[-1]
    step = 32
    for i in range(0, size, step):
        rows = [env_ref[w, i : i + step, :].astype(jnp.float32) for w in range(4)]
        for v in range(4):
            total = rows[0] * weight(p, v, 0)
            for w in range(1, 4):
                total = total + rows[w] * weight(p, v, w)
            mixed_ref[v * size + i : v * size + i + step, :] = total.astype(jnp.bfloat16)
    block = a_ref[pl.ds(pl.multiple_of(p * size, size), size), :]
    half_ref[...] = jnp.dot(
        mixed_ref[...], block, preferred_element_type=jnp.float32
    ).astype(jnp.bfloat16)
    return block


def close(block, half):
    return lax.dot_general(
        block, half, (((0,), (0,)), ((), ())), preferred_element_type=jnp.float32
    )


def one_unit(env_ref, a_ref, weight, p, mixed_ref, half_ref, out_ref):
    size = env_ref.shape[-1]
    block = mix_and_multiply(env_ref, a_ref, weight, p, mixed_ref, half_ref)
    for v in range(4):
        half = half_ref[v * size : (v + 1) * size, :]
        out_ref[v] = close(block, half).astype(jnp.bfloat16)


def listed(w_ref):
    return lambda p, v, w: w_ref[p * 16 + v * 4 + w]


def stay_kernel(w_ref, env_ref, a_ref, out_ref, mixed_ref, half_ref, mixed2_ref, half2_ref):
    size = env_ref.shape[-1]
    weight = listed(w_ref)
    first = mix_and_multiply(env_ref, a_ref, weight, 1, mixed_ref, half_ref)
    second = mix_and_multiply(env_ref, a_ref, weight, 2, mixed2_ref, half2_ref)
    for v in range(4):
        at = slice(v * size, (v + 1) * size)
        total = close(first, half_ref[at, :]) + close(second, half2_ref[at, :])
        out_ref[v] = total.astype(jnp.bfloat16)


def moving_parts(edge, weight, env_ref, a_ref, edge_ref, inner_ref, *work):
    one_unit(env_ref, a_ref, weight, edge, *work[:2], edge_ref)
    one_unit(env_ref, a_ref, weight, 3 - edge, *work[2:], inner_ref)


def first_kernel(
    p_ref, operator_ref, mask_ref, couple_ref, env_any, a_any, edge_ref, inner_ref, env_ref, a_ref, sems, *work
):
    size = env_ref.shape[-1]
    copies = [pltpu.make_async_copy(env_any.at[w], env_ref.at[w], sems.at[w]) for w in range(4)]
    for i, p in enumerate((0, 3)):
        rows = pl.ds(p * size, size)
        copies.append(pltpu.make_async_copy(a_any.at[rows], a_ref.at[rows], sems.at[4 + i]))
    for copy in copies:
        copy.start()
    for copy in copies:
        copy.wait()

    def weight(p, v, w):
        scale = operator_ref[w, v, p] * mask_ref[w, v, p].astype(jnp.float32)
        return scale * couple_ref[p].astype(jnp.float32)

    moving_parts(p_ref[0], weight, env_ref, a_ref, edge_ref, inner_ref, *work)


def summed(cross_ref, swap_ref, stay_ref, env_ref):
    size = env_ref.shape[-1]
    step = 32
    for v in range(4):
        for i in range(0, size, step):
            at = (v, slice(i, i + step))
            total = swap_ref[at].astype(jnp.float32) + stay_ref[at].astype(jnp.float32)
            env_ref[at] = (total + cross_ref[at].astype(jnp.float32)).astype(jnp.bfloat16)


def lead_kernel(
    p_ref, w_ref, cross_ref, swap_ref, stay_ref, a_ref, env_ref, edge_ref, inner_ref, *work
):
    summed(cross_ref, swap_ref, stay_ref, env_ref)
    moving_parts(p_ref[0], listed(w_ref), env_ref, a_ref, edge_ref, inner_ref, *work)


def last_kernel(cross_ref, swap_ref, stay_ref, out_ref):
    summed(cross_ref, swap_ref, stay_ref, out_ref)


def pick_kernel(count, p_ref, *refs):
    out_ref, sem = refs[count], refs[count + 1]
    for i in range(count):

        @pl.when(p_ref[0] == i)
        def _():
            copy = pltpu.make_async_copy(refs[i], out_ref, sem)
            copy.start()
            copy.wait()


VMEM = pl.BlockSpec(memory_space=pltpu.VMEM)
SMEM = pl.BlockSpec(memory_space=pltpu.SMEM)
ANY = pl.BlockSpec(memory_space=pl.ANY)
HBM = pl.BlockSpec(memory_space=pltpu.HBM)
WHOLE = pltpu.CompilerParams(vmem_limit_bytes=64400 * 1024)
PARAMS = pltpu.CompilerParams(vmem_limit_bytes=24 * 1024 * 1024)


def scratch(count, channels, size):
    return [pltpu.VMEM((channels * size, size), jnp.bfloat16)] * count


def cost(units, arrays):
    return pl.CostEstimate(
        flops=units * 8 * 2 * 256**3, bytes_accessed=arrays * 2**19, transcendentals=0
    )


def local(site_blocks, operators, op_mask, coupling, start_env):
    sites = lax.axis_size("site")
    sectors = lax.axis_size("sector")
    row = lax.axis_index("site")
    place = lax.axis_index("sector")
    odd = lax.rem(place, 2)
    states, size = site_blocks.shape[2], site_blocks.shape[3]
    block_shape = jax.ShapeDtypeStruct(start_env.shape[1:], jnp.bfloat16)
    channels = start_env.shape[1]

    def device(position):
        return (0, position) if position >= 0 else (1, position + sites)

    coupled = coupling[0, 0].astype(jnp.float32)
    weights = operators[0] * op_mask[0].astype(jnp.float32) * coupled[None, None, :]
    weights = weights.transpose(2, 1, 0).reshape(-1)
    rooted = jnp.where(row == 0, weights, 0.0)
    blocks = site_blocks[0, 0].reshape(states * size, size)

    def straight_pairs(s):
        return [((s, t), device(t - s)) for t in range(sectors)]

    def turn_pairs(s):
        return [((s, t), (s, (t - s) % sectors)) for t in range(sectors)]

    parcels = {0: blocks, 1: moved(blocks, straight_pairs(1), sectors)}
    scales = {0: rooted}
    for early in (1, 2):
        scales[early] = moved(weights, straight_pairs(early), sectors)
    turned = {}

    def pack(after):
        held, lying, after, scales[1], scales[2] = lax.optimization_barrier(
            (weights, blocks, after, scales[1], scales[2])
        )
        high = lax.reduce_precision(held, *ROUND)
        middle = lax.reduce_precision(held - high, *ROUND)
        low = lax.reduce_precision(held - high - middle, *ROUND)
        pieces = jnp.stack([high, middle, low]).astype(jnp.bfloat16)
        pieces = jnp.pad(pieces, ((0, 13), (0, size - pieces.shape[1])))
        return jnp.concatenate([lying, pieces], axis=0), after

    def weights_of(parcel):
        parts = parcel[states * size : states * size + 3, : weights.shape[0]].astype(jnp.float32)
        return parts[0] + parts[1] + parts[2]

    def fetch(s, after):
        if s not in turned:
            held, after = lax.optimization_barrier((blocks, after))
            return moved(held, straight_pairs(s), sectors), after
        held, after = lax.optimization_barrier((turned[s], after))
        pairs = [((s, (t - s) % sectors), device(t - s)) for t in range(sectors)]
        return moved(held, pairs, sectors), after

    def go_home(r, env):
        pairs = [((r, (t - r) % sectors), (r, t)) for t in range(sectors)]
        return moved(env, pairs, sectors)

    def part_pairs(crossing):
        pairs = []
        for at in range(-sites, sectors):
            to = at - 1 if (at % 2 == 0) == crossing else at + 1
            if -sites <= to < sectors:
                pairs.append((device(at), device(to)))
        return pairs

    control = jnp.stack([3 * odd])
    began = jnp.where(row == 0, coupling[0, 0], 0)
    current = start_env[0]
    homed, raised = {}, {}
    work = scratch(4, channels, size)
    for s in range(sites):
        if s == 0:
            edge, inner = pl.pallas_call(
                first_kernel,
                out_shape=(block_shape,) * 2,
                in_specs=[SMEM] * 4 + [HBM] * 2,
                out_specs=(VMEM,) * 2,
                scratch_shapes=[
                    pltpu.VMEM((channels, size, size), jnp.bfloat16),
                    pltpu.VMEM((states * size, size), jnp.bfloat16),
                    pltpu.SemaphoreType.DMA((6,)),
                ]
                + work,
                compiler_params=WHOLE,
                cost_estimate=cost(2, 4),
                name="first",
            )(control, operators[0], op_mask[0], began, current, blocks)
        else:
            if s not in scales:
                scales[s] = weights_of(parcels[s])
            current, edge, inner = pl.pallas_call(
                lead_kernel,
                out_shape=(block_shape,) * 3,
                in_specs=[SMEM, SMEM] + [VMEM] * 4,
                out_specs=(VMEM,) * 3,
                scratch_shapes=work,
                compiler_params=PARAMS,
                cost_estimate=cost(2, 6),
                name="lead",
            )(control, scales[s], cross, swap, stay, parcels[s])
        cross = moved(edge, part_pairs(True), sectors)
        source = current
        if s == 0:
            source, _ = lax.optimization_barrier((current, edge))
        swap = moved(inner, part_pairs(False), sectors)
        stay = pl.pallas_call(
            stay_kernel,
            out_shape=block_shape,
            in_specs=[SMEM, VMEM, VMEM],
            out_specs=VMEM,
            scratch_shapes=work,
            compiler_params=PARAMS,
            cost_estimate=cost(10, 4),
            name="stay",
        )(scales[s], source, parcels[s])
        if s == 0:
            packed, swap = pack(swap)
            for r in range(3, sites):
                turned[r] = moved(packed, turn_pairs(r), sectors)
        else:
            pairs = [(device(t - s), (s, (t - s) % sectors)) for t in range(sectors)]
            raised[s] = moved(current, pairs, sectors)
        if s - 2 in homed and s < sites - 1:
            stay, homed[s - 2] = lax.optimization_barrier((stay, homed[s - 2]))
        if s - 1 in raised:
            stay, risen = lax.optimization_barrier((stay, raised[s - 1]))
            homed[s - 1] = go_home(s - 1, risen)
        for ahead in (2, 3) if s == 0 else (s + 3,):
            if ahead < sites:
                parcels[ahead], stay = fetch(ahead, stay)

    ended = pl.pallas_call(
        last_kernel,
        out_shape=block_shape,
        in_specs=[VMEM] * 3,
        out_specs=VMEM,
        compiler_params=PARAMS,
        name="last",
    )(cross, swap, stay)
    homed[sites - 1] = go_home(sites - 1, raised[sites - 1])
    homed[0] = moved(ended, [(device(t - sites), (0, t)) for t in range(sectors)], sectors)
    out = pl.pallas_call(
        functools.partial(pick_kernel, sites),
        out_shape=block_shape,
        in_specs=[SMEM, VMEM] + [ANY] * (sites - 1),
        out_specs=VMEM,
        scratch_shapes=[pltpu.SemaphoreType.DMA],
        compiler_params=PARAMS,
        name="pick",
    )(row[None], *[homed[r] for r in range(sites)])
    return out[None, None]


def solution(mesh):
    return jax.shard_map(
        local,
        mesh=mesh,
        in_specs=(
            P("site", "sector", None, None, None),
            P("site", None, None, None),
            P("site", None, None, None),
            P("site", "sector", None),
            P("sector", None, None, None),
        ),
        out_specs=P("site", "sector", None, None, None),
        check_vma=False,
    )
```

```python
import functools

import jax
import jax.numpy as jnp
from jax import lax
from jax.experimental import pallas as pl
from jax.experimental.pallas import tpu as pltpu
from jax.sharding import PartitionSpec as P

AXES = ("site", "sector")
RING = 8
ROUND = (8, 7)


def moved(x, pairs, sectors):
    flat = [(a * sectors + b, c * sectors + d) for (a, b), (c, d) in pairs]
    return lax.ppermute(x, AXES, flat)


def mix_and_multiply(env_ref, a_ref, w_ref, p, mixed_ref, half_ref):
    size = env_ref.shape[-1]
    step = 32
    for i in range(0, size, step):
        rows = [env_ref[w, i : i + step, :].astype(jnp.float32) for w in range(4)]
        for v in range(4):
            total = rows[0] * w_ref[p * 16 + v * 4]
            for w in range(1, 4):
                total = total + rows[w] * w_ref[p * 16 + v * 4 + w]
            mixed_ref[v * size + i : v * size + i + step, :] = total.astype(jnp.bfloat16)
    block = a_ref[pl.ds(pl.multiple_of(p * size, size), size), :]
    half_ref[...] = jnp.dot(
        mixed_ref[...], block, preferred_element_type=jnp.float32
    ).astype(jnp.bfloat16)
    return block


def close(block, half):
    return lax.dot_general(
        block, half, (((0,), (0,)), ((), ())), preferred_element_type=jnp.float32
    )


def one_unit(env_ref, a_ref, w_ref, p, mixed_ref, half_ref, out_ref):
    size = env_ref.shape[-1]
    block = mix_and_multiply(env_ref, a_ref, w_ref, p, mixed_ref, half_ref)
    for v in range(4):
        half = half_ref[v * size : (v + 1) * size, :]
        out_ref[v] = close(block, half).astype(jnp.bfloat16)


def stay_part(env_ref, a_ref, w_ref, mixed_ref, half_ref, mixed2_ref, half2_ref, out_ref):
    size = env_ref.shape[-1]
    first = mix_and_multiply(env_ref, a_ref, w_ref, 1, mixed_ref, half_ref)
    second = mix_and_multiply(env_ref, a_ref, w_ref, 2, mixed2_ref, half2_ref)
    for v in range(4):
        at = slice(v * size, (v + 1) * size)
        total = close(first, half_ref[at, :]) + close(second, half2_ref[at, :])
        out_ref[v] = total.astype(jnp.bfloat16)


def stay_kernel(w_ref, env_ref, a_ref, out_ref, *work):
    stay_part(env_ref, a_ref, w_ref, *work, out_ref)


def moving_parts(p_ref, w_ref, env_ref, a_ref, edge_ref, inner_ref, *work):
    edge = p_ref[0]
    one_unit(env_ref, a_ref, w_ref, edge, *work[:2], edge_ref)
    one_unit(env_ref, a_ref, w_ref, 3 - edge, *work[2:], inner_ref)


def summed(fresh, cross_ref, swap_ref, stay_ref, env_ref):
    size = env_ref.shape[-1]
    step = 32

    def add(refs):
        for v in range(4):
            for i in range(0, size, step):
                at = (v, slice(i, i + step))
                total = refs[0][at].astype(jnp.float32)
                for ref in refs[1:]:
                    total = total + ref[at].astype(jnp.float32)
                env_ref[at] = total.astype(jnp.bfloat16)

    @pl.when(fresh == 1)
    def _():
        add((swap_ref, cross_ref))

    @pl.when(fresh == 0)
    def _():
        add((swap_ref, stay_ref, cross_ref))


def lead_kernel(
    p_ref, w_ref, cross_ref, swap_ref, stay_ref, a_ref, env_ref, edge_ref, inner_ref, *work
):
    summed(p_ref[1], cross_ref, swap_ref, stay_ref, env_ref)
    moving_parts(p_ref, w_ref, env_ref, a_ref, edge_ref, inner_ref, *work)


def last_kernel(count, p_ref, cross_ref, swap_ref, stay_ref, *refs):
    out_ref, sem = refs[count], refs[count + 1]

    @pl.when(p_ref[0] == 0)
    def _():
        summed(p_ref[1], cross_ref, swap_ref, stay_ref, out_ref)

    for i in range(count):

        @pl.when(p_ref[0] == i + 1)
        def _():
            copy = pltpu.make_async_copy(refs[i], out_ref, sem)
            copy.start()
            copy.wait()


def pick_kernel(count, p_ref, *refs):
    out_ref, sem = refs[count], refs[count + 1]
    for i in range(count):

        @pl.when(p_ref[0] == i)
        def _():
            copy = pltpu.make_async_copy(refs[i], out_ref, sem)
            copy.start()
            copy.wait()


VMEM = pl.BlockSpec(memory_space=pltpu.VMEM)
SMEM = pl.BlockSpec(memory_space=pltpu.SMEM)
ANY = pl.BlockSpec(memory_space=pl.ANY)
PARAMS = pltpu.CompilerParams(vmem_limit_bytes=24 * 1024 * 1024)


def scratch(count, channels, size):
    return [pltpu.VMEM((channels * size, size), jnp.bfloat16)] * count


def cost(units, arrays):
    return pl.CostEstimate(
        flops=units * 8 * 2 * 256**3, bytes_accessed=arrays * 2**19, transcendentals=0
    )


def local(site_blocks, operators, op_mask, coupling, start_env):
    sites = lax.axis_size("site")
    sectors = lax.axis_size("sector")
    row = lax.axis_index("site")
    place = lax.axis_index("sector")
    odd = lax.rem(place, 2)
    states, size = site_blocks.shape[2], site_blocks.shape[3]
    block_shape = jax.ShapeDtypeStruct(start_env.shape[1:], jnp.bfloat16)
    channels = start_env.shape[1]

    def device(position):
        return (0, position) if position >= 0 else (1, position + sites)

    def fresh_of(s):
        position = jnp.where(row == 1, place - sites, place)
        return (position + s < 0).astype(jnp.int32)

    coupled = coupling[0, 0].astype(jnp.float32)
    weights = operators[0] * op_mask[0].astype(jnp.float32) * coupled[None, None, :]
    weights = weights.transpose(2, 1, 0).reshape(-1)
    blocks = site_blocks[0, 0].reshape(states * size, size)

    def straight_pairs(s):
        return [((s, t), device(t - s)) for t in range(sectors)]

    early = min(3, sites)
    parcels = {s: moved(blocks, straight_pairs(s), sectors) for s in range(1, early)}
    scales = {s: moved(weights, straight_pairs(s), sectors) for s in range(1, early)}
    parcels[0], scales[0] = blocks, weights

    def pack(after):
        held, lying, after = lax.optimization_barrier((weights, blocks, after))
        high = lax.reduce_precision(held, *ROUND)
        middle = lax.reduce_precision(held - high, *ROUND)
        low = lax.reduce_precision(held - high - middle, *ROUND)
        pieces = jnp.stack([high, middle, low]).astype(jnp.bfloat16)
        pieces = jnp.pad(pieces, ((0, 13), (0, size - pieces.shape[1])))
        packed = jnp.concatenate([lying, pieces], axis=0)
        pairs = [
            ((s, t), (s, (t - s) % sectors)) for s in range(early, sites) for t in range(sectors)
        ]
        return moved(packed, pairs, sectors), after

    def weights_of(parcel):
        parts = parcel[states * size : states * size + 3, : weights.shape[0]].astype(jnp.float32)
        return parts[0] + parts[1] + parts[2]

    def fetch(s, after):
        held, after = lax.optimization_barrier((turned, after))
        pairs = [((s, (t - s) % sectors), device(t - s)) for t in range(sectors)]
        return moved(held, pairs, sectors), after

    def part_pairs(s, crossing):
        pairs = []
        for t in range(sectors):
            at = t - s
            if (at % 2 == 0) == crossing:
                pairs.append((device(at), device(at - 1)))
            elif t + 2 < sectors:
                pairs.append((device(at), device(at + 1)))
        return pairs

    current = start_env[0]
    kept, raised, direct = {}, {}, {}
    work = scratch(4, channels, size)
    late = sites - 1
    for s in range(sites):
        control = jnp.stack([3 * odd, fresh_of(s - 1)])
        if s == 0:
            edge, inner = pl.pallas_call(
                moving_parts,
                out_shape=(block_shape,) * 2,
                in_specs=[SMEM, SMEM, VMEM, VMEM],
                out_specs=(VMEM,) * 2,
                scratch_shapes=work,
                compiler_params=PARAMS,
                cost_estimate=cost(2, 4),
                name="first",
            )(control, scales[0], current, blocks)
        else:
            if s not in scales:
                scales[s] = weights_of(parcels[s])
            current, edge, inner = pl.pallas_call(
                lead_kernel,
                out_shape=(block_shape,) * 3,
                in_specs=[SMEM, SMEM] + [VMEM] * 4,
                out_specs=(VMEM,) * 3,
                scratch_shapes=work,
                compiler_params=PARAMS,
                cost_estimate=cost(2, 6),
                name="lead",
            )(control, scales[s], cross, swap, stay, parcels[s])
            kept[s] = current
        cross = moved(edge, part_pairs(s, True), sectors)
        swap = moved(inner, part_pairs(s, False), sectors)
        if s == 0:
            turned, scales[1] = pack(scales[1])
        stay = pl.pallas_call(
            stay_kernel,
            out_shape=block_shape,
            in_specs=[SMEM, VMEM, VMEM],
            out_specs=VMEM,
            scratch_shapes=work,
            compiler_params=PARAMS,
            cost_estimate=cost(40, 4),
            name="stay",
        )(scales[s], current, parcels[s])
        if s in (1, late):
            direct[s] = moved(kept[s], [(device(t - s), (s, t)) for t in range(sectors)], sectors)
        elif s:
            raised[s] = moved(
                kept[s],
                [(device(t - s), (s, (t - s) % sectors)) for t in range(sectors)],
                sectors,
            )
        if s - 1 in raised and s < late:
            stay, raised[s - 1] = lax.optimization_barrier((stay, raised[s - 1]))
        ahead = s + 2
        if early <= ahead < sites:
            parcels[ahead], stay = fetch(ahead, stay)

    resting = [raised[r] for r in range(2, late)]
    ended = pl.pallas_call(
        functools.partial(last_kernel, len(resting)),
        out_shape=block_shape,
        in_specs=[SMEM] + [VMEM] * 3 + [ANY] * len(resting),
        out_specs=VMEM,
        scratch_shapes=[pltpu.SemaphoreType.DMA],
        compiler_params=PARAMS,
        name="last",
    )(
        jnp.stack([jnp.maximum(row - 1, 0), fresh_of(sites - 1)]),
        cross,
        swap,
        stay,
        *resting,
    )
    pairs = [(device(t - sites), (0, t)) for t in range(sectors)]
    for r in range(2, late):
        pairs += [((r, (t - r) % sectors), (r, t)) for t in range(sectors)]
    home = moved(ended, pairs, sectors)
    out = pl.pallas_call(
        functools.partial(pick_kernel, 3),
        out_shape=block_shape,
        in_specs=[SMEM, VMEM, ANY, ANY],
        out_specs=VMEM,
        scratch_shapes=[pltpu.SemaphoreType.DMA],
        compiler_params=PARAMS,
        name="pick",
    )(
        jnp.stack([jnp.where(row == 1, 1, jnp.where(row == late, 2, 0))]),
        home,
        direct[1],
        direct[late],
    )
    return out[None, None]


def solution(mesh):
    return jax.shard_map(
        local,
        mesh=mesh,
        in_specs=(
            P("site", "sector", None, None, None),
            P("site", None, None, None),
            P("site", None, None, None),
            P("site", "sector", None),
            P("sector", None, None, None),
        ),
        out_specs=P("site", "sector", None, None, None),
        check_vma=False,
    )
```

```python
import functools

import jax
import jax.numpy as jnp
from jax import lax
from jax.experimental import pallas as pl
from jax.experimental.pallas import tpu as pltpu
from jax.sharding import PartitionSpec as P

AXES = ("site", "sector")
RING = 8
ROUND = (8, 7)


def moved(x, pairs, sectors):
    flat = [(a * sectors + b, c * sectors + d) for (a, b), (c, d) in pairs]
    return lax.ppermute(x, AXES, flat)


def mix_and_multiply(env_ref, a_ref, w_ref, p, mixed_ref, half_ref):
    size = env_ref.shape[-1]
    step = 32
    for i in range(0, size, step):
        rows = [env_ref[w, i : i + step, :].astype(jnp.float32) for w in range(4)]
        for v in range(4):
            total = rows[0] * w_ref[p * 16 + v * 4]
            for w in range(1, 4):
                total = total + rows[w] * w_ref[p * 16 + v * 4 + w]
            mixed_ref[v * size + i : v * size + i + step, :] = total.astype(jnp.bfloat16)
    block = a_ref[pl.ds(pl.multiple_of(p * size, size), size), :]
    half_ref[...] = jnp.dot(
        mixed_ref[...], block, preferred_element_type=jnp.float32
    ).astype(jnp.bfloat16)
    return block


def close(block, half):
    return lax.dot_general(
        block, half, (((0,), (0,)), ((), ())), preferred_element_type=jnp.float32
    )


def one_unit(env_ref, a_ref, w_ref, p, mixed_ref, half_ref, out_ref):
    size = env_ref.shape[-1]
    block = mix_and_multiply(env_ref, a_ref, w_ref, p, mixed_ref, half_ref)
    for v in range(4):
        half = half_ref[v * size : (v + 1) * size, :]
        out_ref[v] = close(block, half).astype(jnp.bfloat16)


def stay_part(env_ref, a_ref, w_ref, mixed_ref, half_ref, mixed2_ref, half2_ref, out_ref):
    size = env_ref.shape[-1]
    first = mix_and_multiply(env_ref, a_ref, w_ref, 1, mixed_ref, half_ref)
    second = mix_and_multiply(env_ref, a_ref, w_ref, 2, mixed2_ref, half2_ref)
    for v in range(4):
        at = slice(v * size, (v + 1) * size)
        total = close(first, half_ref[at, :]) + close(second, half2_ref[at, :])
        out_ref[v] = total.astype(jnp.bfloat16)


def stay_kernel(w_ref, env_ref, a_ref, out_ref, *work):
    stay_part(env_ref, a_ref, w_ref, *work, out_ref)


def moving_parts(p_ref, w_ref, env_ref, a_ref, edge_ref, inner_ref, *work):
    edge = p_ref[0]
    one_unit(env_ref, a_ref, w_ref, edge, *work[:2], edge_ref)
    one_unit(env_ref, a_ref, w_ref, 3 - edge, *work[2:], inner_ref)


def summed(fresh, cross_ref, swap_ref, stay_ref, env_ref):
    size = env_ref.shape[-1]
    step = 32

    def add(refs):
        for v in range(4):
            for i in range(0, size, step):
                at = (v, slice(i, i + step))
                total = refs[0][at].astype(jnp.float32)
                for ref in refs[1:]:
                    total = total + ref[at].astype(jnp.float32)
                env_ref[at] = total.astype(jnp.bfloat16)

    @pl.when(fresh == 1)
    def _():
        add((swap_ref, cross_ref))

    @pl.when(fresh == 0)
    def _():
        add((swap_ref, stay_ref, cross_ref))


def lead_kernel(
    p_ref, w_ref, cross_ref, swap_ref, stay_ref, a_ref, env_ref, edge_ref, inner_ref, *work
):
    summed(p_ref[1], cross_ref, swap_ref, stay_ref, env_ref)
    moving_parts(p_ref, w_ref, env_ref, a_ref, edge_ref, inner_ref, *work)


def last_kernel(count, p_ref, cross_ref, swap_ref, stay_ref, *refs):
    out_ref, sem = refs[count], refs[count + 1]

    @pl.when(p_ref[0] == 0)
    def _():
        summed(p_ref[1], cross_ref, swap_ref, stay_ref, out_ref)

    for i in range(count):

        @pl.when(p_ref[0] == i + 1)
        def _():
            copy = pltpu.make_async_copy(refs[i], out_ref, sem)
            copy.start()
            copy.wait()


def pick_kernel(count, p_ref, *refs):
    out_ref, sem = refs[count], refs[count + 1]
    for i in range(count):

        @pl.when(p_ref[0] == i)
        def _():
            copy = pltpu.make_async_copy(refs[i], out_ref, sem)
            copy.start()
            copy.wait()


VMEM = pl.BlockSpec(memory_space=pltpu.VMEM)
SMEM = pl.BlockSpec(memory_space=pltpu.SMEM)
ANY = pl.BlockSpec(memory_space=pl.ANY)
PARAMS = pltpu.CompilerParams(vmem_limit_bytes=24 * 1024 * 1024)


def scratch(count, channels, size):
    return [pltpu.VMEM((channels * size, size), jnp.bfloat16)] * count


def cost(units, arrays):
    return pl.CostEstimate(
        flops=units * 8 * 2 * 256**3, bytes_accessed=arrays * 2**19, transcendentals=0
    )


def local(site_blocks, operators, op_mask, coupling, start_env):
    sites = lax.axis_size("site")
    sectors = lax.axis_size("sector")
    row = lax.axis_index("site")
    place = lax.axis_index("sector")
    odd = lax.rem(place, 2)
    states, size = site_blocks.shape[2], site_blocks.shape[3]
    block_shape = jax.ShapeDtypeStruct(start_env.shape[1:], jnp.bfloat16)
    channels = start_env.shape[1]

    def device(position):
        return (0, position) if position >= 0 else (1, position + sites)

    def fresh_of(s):
        position = jnp.where(row == 1, place - sites, place)
        return (position + s < 0).astype(jnp.int32)

    coupled = coupling[0, 0].astype(jnp.float32)
    weights = operators[0] * op_mask[0].astype(jnp.float32) * coupled[None, None, :]
    weights = weights.transpose(2, 1, 0).reshape(-1)
    blocks = site_blocks[0, 0].reshape(states * size, size)

    def straight_pairs(s):
        return [((s, t), device(t - s)) for t in range(sectors)]

    early = min(3, sites)
    parcels = {s: moved(blocks, straight_pairs(s), sectors) for s in range(1, early)}
    scales = {s: moved(weights, straight_pairs(s), sectors) for s in range(1, early)}
    parcels[0], scales[0] = blocks, weights

    def pack(after):
        held, lying, after = lax.optimization_barrier((weights, blocks, after))
        high = lax.reduce_precision(held, *ROUND)
        middle = lax.reduce_precision(held - high, *ROUND)
        low = lax.reduce_precision(held - high - middle, *ROUND)
        pieces = jnp.stack([high, middle, low]).astype(jnp.bfloat16)
        pieces = jnp.pad(pieces, ((0, 13), (0, size - pieces.shape[1])))
        packed = jnp.concatenate([lying, pieces], axis=0)
        pairs = [
            ((s, t), (s, (t - s) % sectors)) for s in range(early, sites) for t in range(sectors)
        ]
        return moved(packed, pairs, sectors), after

    def weights_of(parcel):
        parts = parcel[states * size : states * size + 3, : weights.shape[0]].astype(jnp.float32)
        return parts[0] + parts[1] + parts[2]

    def fetch(s, after):
        held, after = lax.optimization_barrier((turned, after))
        pairs = [((s, (t - s) % sectors), device(t - s)) for t in range(sectors)]
        return moved(held, pairs, sectors), after

    def part_pairs(s, crossing):
        pairs = []
        for t in range(sectors):
            at = t - s
            if (at % 2 == 0) == crossing:
                pairs.append((device(at), device(at - 1)))
            elif t + 2 < sectors:
                pairs.append((device(at), device(at + 1)))
        return pairs

    current = start_env[0]
    kept, raised, direct = {}, {}, {}
    work = scratch(4, channels, size)
    late = sites - 1
    for s in range(sites):
        control = jnp.stack([3 * odd, fresh_of(s - 1)])
        if s == 0:
            edge, inner = pl.pallas_call(
                moving_parts,
                out_shape=(block_shape,) * 2,
                in_specs=[SMEM, SMEM, VMEM, VMEM],
                out_specs=(VMEM,) * 2,
                scratch_shapes=work,
                compiler_params=PARAMS,
                cost_estimate=cost(2, 4),
                name="first",
            )(control, scales[0], current, blocks)
        else:
            if s not in scales:
                scales[s] = weights_of(parcels[s])
            current, edge, inner = pl.pallas_call(
                lead_kernel,
                out_shape=(block_shape,) * 3,
                in_specs=[SMEM, SMEM] + [VMEM] * 4,
                out_specs=(VMEM,) * 3,
                scratch_shapes=work,
                compiler_params=PARAMS,
                cost_estimate=cost(2, 6),
                name="lead",
            )(control, scales[s], cross, swap, stay, parcels[s])
            kept[s] = current
        cross = moved(edge, part_pairs(s, True), sectors)
        swap = moved(inner, part_pairs(s, False), sectors)
        if s == 0:
            turned, scales[1] = pack(scales[1])
        stay = pl.pallas_call(
            stay_kernel,
            out_shape=block_shape,
            in_specs=[SMEM, VMEM, VMEM],
            out_specs=VMEM,
            scratch_shapes=work,
            compiler_params=PARAMS,
            cost_estimate=cost(40, 4),
            name="stay",
        )(scales[s], current, parcels[s])
        if s in (1, late):
            direct[s] = moved(kept[s], [(device(t - s), (s, t)) for t in range(sectors)], sectors)
        elif s:
            raised[s] = moved(
                kept[s],
                [(device(t - s), (s, (t - s) % sectors)) for t in range(sectors)],
                sectors,
            )
        if s - 1 in raised and s < late:
            stay, raised[s - 1] = lax.optimization_barrier((stay, raised[s - 1]))
        ahead = s + 2
        if early <= ahead < sites:
            parcels[ahead], stay = fetch(ahead, stay)

    ended = pl.pallas_call(
        functools.partial(last_kernel, 0),
        out_shape=block_shape,
        in_specs=[SMEM] + [VMEM] * 3,
        out_specs=VMEM,
        scratch_shapes=[pltpu.SemaphoreType.DMA],
        compiler_params=PARAMS,
        name="last",
    )(jnp.stack([jnp.zeros_like(row), fresh_of(sites - 1)]), cross, swap, stay)
    home = moved(ended, [(device(t - sites), (0, t)) for t in range(sectors)], sectors)
    raised[late - 1], home, direct[1], direct[late] = lax.optimization_barrier(
        (raised[late - 1], home, direct[1], direct[late])
    )
    resting = [raised[r] for r in range(2, late)]
    picked = pl.pallas_call(
        functools.partial(pick_kernel, len(resting)),
        out_shape=block_shape,
        in_specs=[SMEM] + [ANY] * len(resting),
        out_specs=VMEM,
        scratch_shapes=[pltpu.SemaphoreType.DMA],
        compiler_params=PARAMS,
        name="choose",
    )(jnp.stack([row - 2]), *resting)
    pairs = []
    for r in range(2, late):
        pairs += [((r, (t - r) % sectors), (r, t)) for t in range(sectors)]
    homeward = moved(picked, pairs, sectors)
    kind = jnp.where(row == 0, 0, jnp.where(row == 1, 1, jnp.where(row == late, 2, 3)))
    out = pl.pallas_call(
        functools.partial(pick_kernel, 4),
        out_shape=block_shape,
        in_specs=[SMEM, VMEM, ANY, ANY, ANY],
        out_specs=VMEM,
        scratch_shapes=[pltpu.SemaphoreType.DMA],
        compiler_params=PARAMS,
        name="pick",
    )(jnp.stack([kind]), home, direct[1], direct[late], homeward)
    return out[None, None]


def solution(mesh):
    return jax.shard_map(
        local,
        mesh=mesh,
        in_specs=(
            P("site", "sector", None, None, None),
            P("site", None, None, None),
            P("site", None, None, None),
            P("site", "sector", None),
            P("sector", None, None, None),
        ),
        out_specs=P("site", "sector", None, None, None),
        check_vma=False,
    )
```
